32 devices in a mesh: rep: 16 (over z, y, core), shard: 2 (over x).
Axes of the slice: x: 2, y: 2, z: 4, core: 2. Of those that a mesh axis runs over, the one named last changes fastest.
Arguments:
- hidden_in: bfloat16 [4096, 896], P(('rep', 'shard')), may hold values from -6 to 6
- segments: int32 [4096], P(('rep', 'shard')), may hold values from 0 to 15, never falling along the last dimension, each value on 1 to 512 neighbouring positions
- attn_gain: bfloat16 [896], P('shard'), may hold values from 0.5 to 1.5
- w_query: bfloat16 [896, 896], P('shard'), may hold values from -0.1875 to 0.1875
- b_query: bfloat16 [896], P('shard'), may hold values from -3 to 3
- w_key: bfloat16 [896, 128], P('shard'), may hold values from -0.1875 to 0.1875
- b_key: bfloat16 [128], P('shard'), may hold values from -3 to 3
- w_value: bfloat16 [896, 128], P('shard'), may hold values from -0.1875 to 0.1875
- b_value: bfloat16 [128], P('shard'), may hold values from -3 to 3
- w_out: bfloat16 [896, 896], P('shard'), may hold values from -0.75 to 0.75
- mlp_gain: bfloat16 [896], P('shard'), may hold values from 0.5 to 1.5
- w_gate: bfloat16 [896, 4864], P('shard'), may hold values from -0.1875 to 0.1875
- w_up: bfloat16 [896, 4864], P('shard'), may hold values from -0.1875 to 0.1875
- w_down: bfloat16 [4864, 896], P('shard'), may hold values from -0.078125 to 0.078125
- cotangent: bfloat16 [4096, 896], P(('rep', 'shard')), may hold values from -6 to 6
Outputs:
- layer_out: float32 [4096, 896], P(('rep', 'shard'))
- grad_input: float32 [4096, 896], P(('rep', 'shard'))
- grad_attn_gain: float32 [896], P('shard')
- grad_w_query: float32 [896, 896], P('shard')
- grad_b_query: float32 [896], P('shard')
- grad_w_key: float32 [896, 128], P('shard')
- grad_b_key: float32 [128], P('shard')
- grad_w_value: float32 [896, 128], P('shard')
- grad_b_value: float32 [128], P('shard')
- grad_w_out: float32 [896, 896], P('shard')
- grad_mlp_gain: float32 [896], P('shard')
- grad_w_gate: float32 [896, 4864], P('shard')
- grad_w_up: float32 [896, 4864], P('shard')
- grad_w_down: float32 [4864, 896], P('shard')
The draws below stay inside these ranges and needn't reach their ends.
Inputs may be any that keep to these rules, and one draw needn't show every extreme that they name: `segments`: segment numbers never fall along the tokens; each segment holds 1 to 512 tokens and one holds exactly 512.
All inputs are finite; a program needn't handle non-finite values.
Results may differ from the reference program's by a relative error of at most 0.019.
The reference program's roundings to bfloat16 on the way count: a program that leaves them out, or rounds other values in their place, can miss the bound.
Values may be sent and summed in bfloat16 or wider, within the bound.
No kernel may reach another device: no remote copies, remote signals or barrier semaphores. Data moves between devices by JAX's collectives and lax.ppermute only.
A program may use at most 192 MiB of HBM per device.

```python
import math
import jax
import jax.numpy as jnp
import numpy as np
from jax import lax

D = 896
HEADS = 14
KV_HEADS = 2
HEAD_DIM = 64
FF = 4864
SEQ = 512
TOKENS = 4096


def steps_of(own_key, extent, pieces, least, high):
    def one(position, shards_of):
        steps = jax.random.uniform(jax.random.fold_in(jax.random.fold_in(own_key, 6), position), (shards_of,), jnp.float32, least / len(pieces), high / len(pieces))
        return jnp.repeat(jnp.exp(steps), extent[position] // shards_of).reshape((-1,) + (1,) * (len(extent) - position - 1))

    factor_of = one(*pieces[0])
    for cut in pieces[1:]:
        factor_of = factor_of * one(*cut)
    return factor_of


def profile(count, total, limit, lean):
    loads = [(1 << 20) // math.isqrt(rank ** lean) + 1 for rank in range(2, count + 1)]
    surplus, given = total - limit - (count - 1), [1] * (count - 1)
    while surplus > 0:
        movable = [i for i in range(count - 1) if given[i] < limit]
        whole, left = sum([loads[i] for i in movable]), surplus
        for i in movable:
            extra = min(limit - given[i], max(1, left * loads[i] // whole), surplus)
            given[i] = given[i] + extra
            surplus = surplus - extra
    return np.array([limit] + given)


def uneven_parts(rng, count, total, most, lean):
    if count == 2:
        one = jax.random.randint(rng, (), max(1, total - most), min(most, total - 1) + 1)
        return jnp.stack([one, total - one])
    lengths = jnp.asarray(profile(count, total, most, lean), jnp.int32)
    pairs = (count - 1) // 2
    donor, taker = lengths[1:1 + 2 * pairs:2], lengths[2:2 + 2 * pairs:2]
    margin = jnp.minimum(donor - 1, most - taker)
    moved = jax.random.randint(jax.random.fold_in(rng, 1), (pairs,), 0, 1 << 20) % (margin + 1)
    lengths = lengths.at[1:1 + 2 * pairs:2].set(donor - moved).at[2:2 + 2 * pairs:2].set(taker + moved)
    return lengths[jax.random.permutation(jax.random.fold_in(rng, 2), count)]


def bell_draw(key, dims, deviation, reach, pieces=(), held_as=jnp.bfloat16):
    drawn = jax.random.normal(key, dims, jnp.float32) * deviation
    if len(pieces) > 0:
        drawn = steps_of(key, dims, pieces, -0.22, 0.18) * drawn
    return jnp.clip(drawn, min=-reach, max=reach).astype(held_as)


def setup_inputs(seed: int = 0) -> dict:
    seeds = jax.random.split(jax.random.key(seed), 16)
    return {
        "hidden_in": bell_draw(seeds[0], (TOKENS, D), 1.0, 6.0, ((0, 32),)),
        "segments": jnp.searchsorted(jnp.cumsum(uneven_parts(seeds[1], 2 * TOKENS // SEQ, TOKENS, SEQ, 0)), jnp.arange(TOKENS), side="right").astype(jnp.int32),
        "attn_gain": jnp.clip(1.0 + 0.1 * jax.random.normal(seeds[2], (D,), jnp.float32), 0.5, 1.5).astype(jnp.bfloat16),
        "w_query": bell_draw(seeds[3], (D, D), D ** -0.5, 0.1875, ((0, 2),)),
        "b_query": bell_draw(seeds[4], (D,), 0.5, 3.0, ((0, 2),)),
        "w_key": bell_draw(seeds[5], (D, KV_HEADS * HEAD_DIM), D ** -0.5, 0.1875, ((0, 2),)),
        "b_key": bell_draw(seeds[6], (KV_HEADS * HEAD_DIM,), 0.5, 3.0, ((0, 2),)),
        "w_value": bell_draw(seeds[7], (D, KV_HEADS * HEAD_DIM), D ** -0.5, 0.1875, ((0, 2),)),
        "b_value": bell_draw(seeds[8], (KV_HEADS * HEAD_DIM,), 0.5, 3.0, ((0, 2),)),
        "w_out": bell_draw(seeds[9], (D, D), (max(D // 16, 1)) ** -0.5, 0.75, ((0, 2),)),
        "mlp_gain": jnp.clip(1.0 + 0.1 * jax.random.normal(seeds[10], (D,), jnp.float32), 0.5, 1.5).astype(jnp.bfloat16),
        "w_gate": bell_draw(seeds[11], (D, FF), D ** -0.5, 0.1875, ((0, 2),)),
        "w_up": bell_draw(seeds[12], (D, FF), D ** -0.5, 0.1875, ((0, 2),)),
        "w_down": bell_draw(seeds[13], (FF, D), FF ** -0.5, 0.078125, ((0, 2),)),
        "cotangent": bell_draw(seeds[14], (TOKENS, D), 1.0, 6.0, ((0, 32),)),
    }


EPSILON = 1e-06
ROPE_THETA = 1000000.0
MASKED = -1e+30

def rounded(values):
    return lax.optimization_barrier(values.astype(jnp.bfloat16))

def rope_tables(positions):
    half_width = HEAD_DIM // 2
    inverse = ROPE_THETA ** (-(jnp.arange(half_width, dtype=jnp.float32) * 2.0) / HEAD_DIM)
    angle_half = positions.astype(jnp.float32)[:, None] * inverse[None, :]
    angle_full = jnp.concatenate([angle_half, angle_half], axis=-1)
    return (jnp.cos(angle_full), jnp.sin(angle_full))

def rotate_half(values):
    half_width = values.shape[-1] // 2
    return jnp.concatenate([-values[..., half_width:], values[..., :half_width]], axis=-1)

def rotate_back(values):
    half_width = values.shape[-1] // 2
    return jnp.concatenate([values[..., half_width:], -values[..., :half_width]], axis=-1)

def apply_rope(values, cosine, sine_table):
    return values * cosine[:, None, :] + rotate_half(values) * sine_table[:, None, :]

def undo_rope(grads, cosine, sine_table):
    return grads * cosine[:, None, :] + rotate_back(grads * sine_table[:, None, :])

def rms_forward(values, gain):
    inv_scale = lax.rsqrt(lax.optimization_barrier(jnp.mean(values * values, axis=-1, keepdims=True)) + EPSILON)
    normed = values * inv_scale
    return (normed, inv_scale, normed * gain)

def rms_backward(grads, normed, inv_scale, gain):
    through = grads * gain
    inner = lax.optimization_barrier(jnp.mean(through * normed, axis=-1, keepdims=True))
    return (inv_scale * (through - normed * inner), lax.optimization_barrier(jnp.sum(grads * normed, axis=0)))

def attend(queries, keys_win, values_win, allowed):
    scale = 1.0 / math.sqrt(HEAD_DIM)
    scores = jnp.einsum('qkgd,wkd->kgqw', queries.astype(jnp.float32), keys_win.astype(jnp.float32)) * scale
    scores = jnp.where(allowed[None, None], scores, MASKED)
    row_max = lax.optimization_barrier(jnp.max(scores, axis=-1, keepdims=True))
    raw_weights = jnp.exp(scores - row_max)
    row_total = lax.optimization_barrier(jnp.sum(raw_weights, axis=-1, keepdims=True))
    soft_probs = rounded(raw_weights / row_total)
    log_total = row_max + jnp.log(row_total)
    output = jnp.einsum('kgqw,wkd->qkgd', soft_probs.astype(jnp.float32), values_win.astype(jnp.float32))
    return (rounded(output), log_total)

def attend_back(queries, keys_win, values_win, allowed, out_rows, grad_rows, log_total):
    scale = 1.0 / math.sqrt(HEAD_DIM)
    scores = jnp.einsum('qkgd,wkd->kgqw', queries.astype(jnp.float32), keys_win.astype(jnp.float32)) * scale
    scores = jnp.where(allowed[None, None], scores, MASKED)
    soft_probs = jnp.exp(scores - log_total)
    probs_low = rounded(soft_probs)
    grad_values = jnp.einsum('kgqw,qkgd->wkd', probs_low.astype(jnp.float32), grad_rows.astype(jnp.float32))
    grad_probs = jnp.einsum('qkgd,wkd->kgqw', grad_rows.astype(jnp.float32), values_win.astype(jnp.float32))
    delta = lax.optimization_barrier(jnp.sum(grad_rows.astype(jnp.float32) * out_rows.astype(jnp.float32), axis=-1))
    delta = jnp.transpose(delta, (1, 2, 0))[..., None]
    grad_scores = rounded(soft_probs * (grad_probs - delta) * scale)
    grad_queries = jnp.einsum('kgqw,wkd->qkgd', grad_scores.astype(jnp.float32), keys_win.astype(jnp.float32))
    grad_keys = jnp.einsum('kgqw,qkgd->wkd', grad_scores.astype(jnp.float32), queries.astype(jnp.float32))
    return (grad_queries, grad_keys, grad_values)

def reference(hidden_in, segments, attn_gain, w_query, b_query, w_key, b_key, w_value, b_value, w_out, mlp_gain, w_gate, w_up, w_down, cotangent):
    head_group = HEADS // KV_HEADS
    kv_width = KV_HEADS * HEAD_DIM
    token_index = jnp.arange(TOKENS, dtype=jnp.int32)
    previous = jnp.concatenate([jnp.full((1,), -1, jnp.int32), segments[:-1]])
    seg_start = lax.cummax(jnp.where(segments != previous, token_index, jnp.zeros_like(token_index)), axis=0)
    positions = token_index - seg_start
    cosine, sine_table = rope_tables(positions)
    input_wide = hidden_in.astype(jnp.float32)
    gain_attn = attn_gain.astype(jnp.float32)
    gain_mlp = mlp_gain.astype(jnp.float32)
    normed_attn, inv_attn, scaled_attn = rms_forward(input_wide, gain_attn)
    attn_input = rounded(scaled_attn)
    query_lin = jnp.dot(attn_input, w_query, preferred_element_type=jnp.float32) + b_query.astype(jnp.float32)
    key_lin = jnp.dot(attn_input, w_key, preferred_element_type=jnp.float32) + b_key.astype(jnp.float32)
    value_lin = jnp.dot(attn_input, w_value, preferred_element_type=jnp.float32) + b_value.astype(jnp.float32)
    query_rot = rounded(apply_rope(query_lin.reshape(TOKENS, HEADS, HEAD_DIM), cosine, sine_table))
    key_rot = rounded(apply_rope(key_lin.reshape(TOKENS, KV_HEADS, HEAD_DIM), cosine, sine_table))
    value_low = rounded(value_lin.reshape(TOKENS, KV_HEADS, HEAD_DIM))
    block_len = 512 if TOKENS % 512 == 0 else TOKENS
    block_count = TOKENS // block_len
    window = block_len + SEQ
    key_pad = jnp.concatenate([jnp.zeros((SEQ, KV_HEADS, HEAD_DIM), jnp.bfloat16), key_rot], axis=0)
    value_pad = jnp.concatenate([jnp.zeros((SEQ, KV_HEADS, HEAD_DIM), jnp.bfloat16), value_low], axis=0)
    seg_pad = jnp.concatenate([jnp.full((SEQ,), -1, jnp.int32), segments], axis=0)

    def window_of(block_id):
        first_row = (block_id * block_len).astype(jnp.int32)
        queries = lax.dynamic_slice_in_dim(query_rot, first_row, block_len, 0).reshape(block_len, KV_HEADS, head_group, HEAD_DIM)
        keys_win = lax.dynamic_slice_in_dim(key_pad, first_row, window, 0)
        values_win = lax.dynamic_slice_in_dim(value_pad, first_row, window, 0)
        seg_win = lax.dynamic_slice_in_dim(seg_pad, first_row, window, 0)
        seg_rows = lax.dynamic_slice_in_dim(segments, first_row, block_len, 0)
        query_at = first_row + jnp.arange(block_len, dtype=jnp.int32)
        key_at = first_row - SEQ + jnp.arange(window, dtype=jnp.int32)
        allowed = (seg_rows[:, None] == seg_win[None, :]) & (key_at[None, :] <= query_at[:, None])
        return (queries, keys_win, values_win, allowed)

    def forward_block(block_id):
        queries, keys_win, values_win, allowed = window_of(block_id)
        output, log_total = attend(queries, keys_win, values_win, allowed)
        return (output.reshape(block_len, D), log_total)
    block_ids = jnp.arange(block_count, dtype=jnp.int32)
    attn_blocks, log_totals = lax.map(forward_block, block_ids)
    attn_out = attn_blocks.reshape(TOKENS, D)
    after_attn = input_wide + jnp.dot(attn_out, w_out, preferred_element_type=jnp.float32)
    mlp_len = 4096 if TOKENS % 4096 == 0 else TOKENS

    def mlp_step(running, inputs):
        resid_rows, cot_rows = inputs
        normed_mlp, inv_mlp, scaled_mlp = rms_forward(resid_rows, gain_mlp)
        mlp_input = rounded(scaled_mlp)
        gate_lin = jnp.dot(mlp_input, w_gate, preferred_element_type=jnp.float32)
        up_lin = jnp.dot(mlp_input, w_up, preferred_element_type=jnp.float32)
        gate_sig = jax.nn.sigmoid(gate_lin)
        gate_act = gate_lin * gate_sig
        hidden_low = rounded(gate_act * up_lin)
        block_out = resid_rows + jnp.dot(hidden_low, w_down, preferred_element_type=jnp.float32)
        grad_hidden = jnp.dot(cot_rows, w_down.T, preferred_element_type=jnp.float32)
        grad_gate_lin = rounded(grad_hidden * up_lin * gate_sig * (1.0 + gate_lin * (1.0 - gate_sig)))
        grad_up_lin = rounded(grad_hidden * gate_act)
        grad_normed = jnp.dot(grad_gate_lin, w_gate.T, preferred_element_type=jnp.float32) + jnp.dot(grad_up_lin, w_up.T, preferred_element_type=jnp.float32)
        grad_part, gain_term = rms_backward(grad_normed, normed_mlp, inv_mlp, gain_mlp)
        acc_gate, acc_up, acc_down, acc_gain = running
        acc_gate = acc_gate + jnp.dot(mlp_input.T, grad_gate_lin, preferred_element_type=jnp.float32)
        acc_up = acc_up + jnp.dot(mlp_input.T, grad_up_lin, preferred_element_type=jnp.float32)
        acc_down = acc_down + jnp.dot(hidden_low.T, cot_rows, preferred_element_type=jnp.float32)
        acc_gain = acc_gain + gain_term
        return ((acc_gate, acc_up, acc_down, acc_gain), (block_out, cot_rows.astype(jnp.float32) + grad_part))
    mlp_init = (jnp.zeros((D, FF), jnp.float32), jnp.zeros((D, FF), jnp.float32), jnp.zeros((FF, D), jnp.float32), jnp.zeros((D,), jnp.float32))
    mlp_sums, mlp_rows = lax.scan(mlp_step, mlp_init, (after_attn.reshape(-1, mlp_len, D), cotangent.reshape(-1, mlp_len, D)))
    grad_w_gate, grad_w_up, grad_w_down, grad_mlp_gain = mlp_sums
    layer_out = mlp_rows[0].reshape(TOKENS, D)
    grad_after = mlp_rows[1].reshape(TOKENS, D)
    after_low = rounded(grad_after)
    grad_w_out = jnp.dot(attn_out.T, after_low, preferred_element_type=jnp.float32)
    grad_attn_out = rounded(jnp.dot(after_low, w_out.T, preferred_element_type=jnp.float32))

    def backward_block(running, block_id):
        key_acc, value_acc = running
        queries, keys_win, values_win, allowed = window_of(block_id)
        first_row = (block_id * block_len).astype(jnp.int32)
        out_rows = lax.dynamic_slice_in_dim(attn_out, first_row, block_len, 0).reshape(block_len, KV_HEADS, head_group, HEAD_DIM)
        grad_rows = lax.dynamic_slice_in_dim(grad_attn_out, first_row, block_len, 0).reshape(block_len, KV_HEADS, head_group, HEAD_DIM)
        grad_queries, grad_keys, grad_values = attend_back(queries, keys_win, values_win, allowed, out_rows, grad_rows, log_totals[block_id])
        key_acc = lax.dynamic_update_slice_in_dim(key_acc, lax.dynamic_slice_in_dim(key_acc, first_row, window, 0) + grad_keys, first_row, 0)
        value_acc = lax.dynamic_update_slice_in_dim(value_acc, lax.dynamic_slice_in_dim(value_acc, first_row, window, 0) + grad_values, first_row, 0)
        return ((key_acc, value_acc), grad_queries.reshape(block_len, HEADS, HEAD_DIM))
    back_init = (jnp.zeros((SEQ + TOKENS, KV_HEADS, HEAD_DIM), jnp.float32), jnp.zeros((SEQ + TOKENS, KV_HEADS, HEAD_DIM), jnp.float32))
    back_sums, grad_query_blocks = lax.scan(backward_block, back_init, block_ids)
    grad_query_rot = grad_query_blocks.reshape(TOKENS, HEADS, HEAD_DIM)
    grad_key_rot = back_sums[0][SEQ:]
    grad_value_lin = back_sums[1][SEQ:].reshape(TOKENS, kv_width)
    grad_query_lin = undo_rope(grad_query_rot, cosine, sine_table).reshape(TOKENS, D)
    grad_key_lin = undo_rope(grad_key_rot, cosine, sine_table).reshape(TOKENS, kv_width)
    grad_b_query = lax.optimization_barrier(jnp.sum(grad_query_lin, axis=0))
    grad_b_key = lax.optimization_barrier(jnp.sum(grad_key_lin, axis=0))
    grad_b_value = lax.optimization_barrier(jnp.sum(grad_value_lin, axis=0))
    query_low = rounded(grad_query_lin)
    key_low = rounded(grad_key_lin)
    value_grad_low = rounded(grad_value_lin)
    grad_w_query = jnp.dot(attn_input.T, query_low, preferred_element_type=jnp.float32)
    grad_w_key = jnp.dot(attn_input.T, key_low, preferred_element_type=jnp.float32)
    grad_w_value = jnp.dot(attn_input.T, value_grad_low, preferred_element_type=jnp.float32)
    grad_attn_normed = jnp.dot(query_low, w_query.T, preferred_element_type=jnp.float32) + jnp.dot(key_low, w_key.T, preferred_element_type=jnp.float32) + jnp.dot(value_grad_low, w_value.T, preferred_element_type=jnp.float32)
    grad_part, grad_attn_gain = rms_backward(grad_attn_normed, normed_attn, inv_attn, gain_attn)
    grad_input = grad_after + grad_part
    return (layer_out, grad_input, grad_attn_gain, grad_w_query, grad_b_query, grad_w_key, grad_b_key, grad_w_value, grad_b_value, grad_w_out, grad_mlp_gain, grad_w_gate, grad_w_up, grad_w_down)
```

```python
import math

import jax
import jax.numpy as jnp
from jax import lax
from jax.experimental import pallas as pl
from jax.experimental.pallas import tpu as pltpu
from jax.sharding import PartitionSpec as P

D = 896
HEADS = 14
KV_HEADS = 2
HEAD_DIM = 64
SEQ = 512


EPSILON = 1e-06
ROPE_THETA = 1000000.0
MASKED = -1e30

CORES = 2
ALONG_Z = 4


def passed_along(shard, axis, by):
    peers = lax.axis_size(axis)
    pairs = [(i, i + by) for i in range(peers) if 0 <= i + by < peers]
    return lax.ppermute(shard, axis, pairs)


def rep_sizes():
    planes = lax.axis_size("rep") // CORES
    zs = min(ALONG_Z, planes)
    return (zs, planes // zs)


def own_place():
    zs, ys = rep_sizes()
    rep = lax.axis_index("rep")
    plane = rep // CORES
    return {"z": plane // ys, "y": plane % ys, "core": rep % CORES, "shard": lax.axis_index("shard")}


def steps_of(axis):
    zs, ys = rep_sizes()
    size = {"z": zs, "y": ys, "core": CORES, "shard": lax.axis_size("shard")}[axis]
    return [(axis, 1 << i) for i in range(size.bit_length() - 1)]


def swap(value, step):
    axis, bit = step
    if axis == "shard":
        peers = lax.axis_size("shard")
        return lax.ppermute(value, "shard", [(i, i ^ bit) for i in range(peers)])
    zs, ys = rep_sizes()
    pairs = []
    for rep in range(zs * ys * CORES):
        at = {"z": rep // CORES // ys, "y": rep // CORES % ys, "core": rep % CORES}
        at[axis] ^= bit
        pairs.append((rep, (at["z"] * ys + at["y"]) * CORES + at["core"]))
    return lax.ppermute(value, "rep", pairs)


def own_bit(place, step):
    return place[step[0]] // step[1] % 2


def nothing(*refs):
    pass


def after(value, *earlier):
    anywhere = pl.BlockSpec(memory_space=pl.ANY)
    return pl.pallas_call(
        nothing,
        out_shape=jax.ShapeDtypeStruct(value.shape, value.dtype),
        in_specs=[anywhere] * (1 + len(earlier)),
        out_specs=anywhere,
        input_output_aliases={0: 0},
        cost_estimate=pl.CostEstimate(flops=0, bytes_accessed=0, transcendentals=0),
        name="after",
    )(value, *earlier)


def pick(whole, at, axis=0):
    return lax.dynamic_index_in_dim(whole, at, axis, keepdims=False)


def ordered(mine, got, place, step, axis=0):
    first = own_bit(place, step) == 0
    return jnp.where(
        first, jnp.concatenate([mine, got], axis=axis), jnp.concatenate([got, mine], axis=axis)
    )


def gather(piece, place, steps):
    for step in steps:
        piece = ordered(piece, swap(piece, step), place, step)
    return piece


def scatter_step(parts, place, step, axis=0, earlier=()):
    at = own_bit(place, step)
    got = swap(pick(parts, 1 - at, axis), step)
    if earlier:
        got = after(got, *earlier)
    total = pick(parts, at, axis).astype(jnp.float32) + got.astype(jnp.float32)
    return total.astype(jnp.bfloat16)


def scatter(parts, place, steps, lead=0, earlier=()):
    for index, step in enumerate(steps):
        parts = scatter_step(
            parts, place, step, lead + len(steps) - 1 - index, earlier[index : index + 1]
        )
    return parts


def exchange(parts, place, earlier):
    shards = lax.axis_size("shard")
    if shards == 2:
        at = place["shard"]
        got = after(swap(pick(parts, 1 - at), ("shard", 1)), earlier)
        return ordered(pick(parts, at)[None], got[None], place, ("shard", 1))
    return lax.all_to_all(parts, "shard", split_axis=0, concat_axis=0, tiled=True)


def group_tokens(rows, steps):
    for step in steps:
        rows = jnp.concatenate([rows, swap(rows, step)], axis=0)
    return rows


def group_step(parts, step, earlier=()):
    half = parts.shape[0] // 2
    sent = parts[half:]
    if step[0] != "core":
        sent = sent.astype(jnp.bfloat16)
    got = swap(sent, step)
    if earlier:
        got = after(got, *earlier)
    return parts[:half] + got.astype(jnp.float32)


def group_sum(parts, steps):
    for step in steps[::-1]:
        parts = group_step(parts, step)
    return parts


def sum_everywhere(value):
    for axis in ("core", "shard", "y", "z"):
        for step in steps_of(axis):
            value = value + swap(value, step)
    return value


def rope_tables(positions):
    half_width = HEAD_DIM // 2
    inverse = ROPE_THETA ** (-(jnp.arange(half_width, dtype=jnp.float32) * 2.0) / HEAD_DIM)
    angle_half = positions.astype(jnp.float32)[:, None] * inverse[None, :]
    angle_full = jnp.concatenate([angle_half, angle_half], axis=-1)
    return (jnp.cos(angle_full), jnp.sin(angle_full))


def rotate_half(values):
    half_width = values.shape[-1] // 2
    return jnp.concatenate([-values[..., half_width:], values[..., :half_width]], axis=-1)


def rotate_back(values):
    half_width = values.shape[-1] // 2
    return jnp.concatenate([values[..., half_width:], -values[..., :half_width]], axis=-1)


def apply_rope(values, cosine, sine_table):
    return values * cosine[:, None, :] + rotate_half(values) * sine_table[:, None, :]


def undo_rope(grads, cosine, sine_table):
    return grads * cosine[:, None, :] + rotate_back(grads * sine_table[:, None, :])


def rms_forward(values, gain):
    inv_scale = lax.rsqrt(jnp.mean(values * values, axis=-1, keepdims=True) + EPSILON)
    normed = values * inv_scale
    return (normed, inv_scale, normed * gain)


def rms_backward(grads, normed, inv_scale, gain):
    through = grads * gain
    inner = jnp.mean(through * normed, axis=-1, keepdims=True)
    return (inv_scale * (through - normed * inner), jnp.sum(grads * normed, axis=0))


def spans(first, count, size):
    cuts = []
    at = first
    while at < first + count:
        end = min((at // size + 1) * size, first + count)
        cuts.append((at // size, at % size, at - first, end - at))
        at = end
    return cuts


def kept_of(index, ff_block, ff_own):
    at = min(index * ff_block, ff_own - ff_block)
    return (at, min(index * ff_block - at, ff_block))


def weight_sums(mlp_rows, cot_rows, hidden_low, grad_gate, grad_up, zs, shards):
    tokens, width = mlp_rows.shape
    units = hidden_low.shape[1]
    rows = width // zs
    d_z = width // shards // zs
    f_z = units // zs

    def kernel(x_ref, cot_ref, hidden_ref, gate_ref, up_ref, out_ref):
        def column_sum(left_ref, first, right_ref):
            return lax.dot_general(
                left_ref[:, first : first + 128],
                right_ref[...],
                (((0,), (0,)), ((), ())),
                preferred_element_type=jnp.float32,
            ).astype(jnp.bfloat16)

        for first in range(0, units, 128):
            got = column_sum(hidden_ref, first, cot_ref)
            for z, row, at, count in spans(first, 128, f_z):
                for tile in range(width // 128):
                    piece = got[at : at + count, tile * 128 : (tile + 1) * 128]
                    for to, to_row, from_row, length in spans(tile * f_z + row, count, rows):
                        out_ref[z, 0, to_row : to_row + length, to * 128 : (to + 1) * 128] = piece[
                            from_row : from_row + length
                        ]
        for index, right_ref in ((1, gate_ref), (2, up_ref)):
            for first in range(0, width, 128):
                got = column_sum(x_ref, first, right_ref)
                for part, row, at, count in spans(first, 128, d_z):
                    to_row = part // zs * d_z + row
                    out_ref[part % zs, index, to_row : to_row + count] = got[at : at + count]

    operands = (mlp_rows, cot_rows, hidden_low, grad_gate, grad_up)
    return pl.pallas_call(
        kernel,
        out_shape=jax.ShapeDtypeStruct((zs, 3, rows, units), jnp.bfloat16),
        in_specs=[pl.BlockSpec(memory_space=pltpu.VMEM)] * 5,
        out_specs=pl.BlockSpec(memory_space=pltpu.VMEM),
        compiler_params=pltpu.CompilerParams(vmem_limit_bytes=48 * 1024 * 1024),
        cost_estimate=pl.CostEstimate(
            flops=6 * tokens * width * units, bytes_accessed=12 * 1024 * 1024, transcendentals=0
        ),
        name="weight_sums",
    )(*operands)


def weights_in_place(all_all, shards, ff_own):
    zs, blocks, _, rows, units = all_all.shape
    width = rows * zs
    d_z = rows // shards
    f_z = units // zs

    def kernel(all_ref, gate_ref, up_ref, down_ref, wide_ref, sems):
        z = pl.program_id(0)
        for index in range(blocks):
            for tile in range(width // 128):
                for part, row, at, count in spans(tile * f_z, f_z, rows):
                    wide_ref[index, at : at + count, tile * 128 : (tile + 1) * 128] = all_ref[
                        0, index, 0, row : row + count, part * 128 : (part + 1) * 128
                    ].astype(jnp.float32)

        def move(index, skip):
            at = kept_of(index, units, ff_own)[0]
            to = pl.multiple_of(at + z * f_z + skip, 8)
            return pltpu.make_async_copy(
                wide_ref.at[index, pl.ds(skip, f_z - skip)],
                down_ref.at[pl.ds(to, f_z - skip)],
                sems.at[index],
            )

        def each_move(act):
            for index in range(blocks):
                dropped = kept_of(index, units, ff_own)[1]
                for place in range(zs):
                    skip = min(max(dropped - place * f_z, 0), f_z)
                    if skip < f_z:

                        @pl.when(z == place)
                        def _(index=index, skip=skip):
                            act(move(index, skip))

        each_move(lambda copy: copy.start())
        for number, out_ref in ((1, gate_ref), (2, up_ref)):
            for owner in range(shards):
                for index in range(blocks):
                    at, skip = kept_of(index, units, ff_own)
                    if skip < units:
                        out_ref[:, owner * ff_own + at + skip : owner * ff_own + at + units] = all_ref[
                            0, index, number, owner * d_z : (owner + 1) * d_z, skip:
                        ].astype(jnp.float32)
        each_move(lambda copy: copy.wait())

    wide = jax.ShapeDtypeStruct((d_z * zs, shards * ff_own), jnp.float32)
    return pl.pallas_call(
        kernel,
        grid=(zs,),
        out_shape=(wide, wide, jax.ShapeDtypeStruct((ff_own, width), jnp.float32)),
        in_specs=[pl.BlockSpec((1, blocks, 3, rows, units), lambda z: (z, 0, 0, 0, 0))],
        out_specs=(
            pl.BlockSpec((d_z, shards * ff_own), lambda z: (z, 0)),
            pl.BlockSpec((d_z, shards * ff_own), lambda z: (z, 0)),
            pl.BlockSpec(memory_space=pl.ANY),
        ),
        scratch_shapes=[
            pltpu.VMEM((blocks, f_z, width), jnp.float32),
            pltpu.SemaphoreType.DMA((blocks,)),
        ],
        compiler_params=pltpu.CompilerParams(vmem_limit_bytes=48 * 1024 * 1024),
        cost_estimate=pl.CostEstimate(flops=0, bytes_accessed=44 * 1024 * 1024, transcendentals=0),
        name="weights_in_place",
    )(all_all)


def prior_rows(rows, back_reach):
    parts = []
    for distance in range(back_reach, 0, -1):
        parts.append(passed_along(rows, ("rep", "shard"), distance))
    parts.append(rows)
    return jnp.concatenate(parts, axis=0)


def return_rows(grads, tok_rows, back_reach):
    total = grads[back_reach * tok_rows :]
    for distance in range(back_reach, 0, -1):
        first_row = (back_reach - distance) * tok_rows
        total = total + passed_along(
            grads[first_row : first_row + tok_rows], ("rep", "shard"), -distance
        )
    return total


def token_sum(left, right):
    return lax.dot_general(
        left, right, (((0,), (0,)), ((), ())), preferred_element_type=jnp.float32
    ).astype(jnp.bfloat16)


def per_device(
    hidden_in,
    segments,
    attn_gain,
    w_query,
    b_query,
    w_key,
    b_key,
    w_value,
    b_value,
    w_out,
    mlp_gain,
    w_gate,
    w_up,
    w_down,
    cotangent,
):
    tok_rows = hidden_in.shape[0]
    back_reach = (SEQ - 2) // tok_rows + 1
    head_group = HEADS // KV_HEADS
    kv_width = KV_HEADS * HEAD_DIM
    qkv_width = D + 2 * kv_width
    scale = 1.0 / math.sqrt(HEAD_DIM)
    place = own_place()
    core, shard = place["core"], place["shard"]
    shards = lax.axis_size("shard")
    zs, ys = rep_sizes()
    d_own = D // shards
    shard_steps, y_steps, z_steps, core_steps = [
        steps_of(axis) for axis in ("shard", "y", "z", "core")
    ]
    group_steps = shard_steps + y_steps + core_steps

    ff_own = w_down.shape[0]
    blocks = ys * CORES
    ff_block = min(ff_own, -(-ff_own // (blocks * 128)) * 128)
    block = place["y"] * CORES + core
    block_at = jnp.minimum(block * ff_block, ff_own - ff_block)

    w_qkv = jnp.concatenate([w_query, w_key, w_value], axis=1)
    qkv_half = pick(w_qkv.reshape(CORES, d_own // CORES, qkv_width), core)
    own_segments = after(segments, qkv_half) + 1
    ext_segments = prior_rows(own_segments, back_reach)
    small = jnp.concatenate([attn_gain, b_query, b_key, b_value, mlp_gain])
    small_all = gather(after(small, qkv_half)[None], place, shard_steps)
    kv_own = kv_width // shards
    cuts = [0, d_own, 2 * d_own, 2 * d_own + kv_own, 2 * d_own + 2 * kv_own, small.shape[0]]
    gain_low, bias_query, bias_key, bias_value, mlp_low = [
        small_all[:, a:b].reshape(-1) for a, b in zip(cuts[:-1], cuts[1:])
    ]
    bias_qkv = jnp.concatenate([bias_query, bias_key, bias_value]).astype(jnp.float32)

    ext_len = ext_segments.shape[0]
    column = jnp.arange(ext_len, dtype=jnp.int32)
    row_at = back_reach * tok_rows + jnp.arange(tok_rows, dtype=jnp.int32)
    same_doc = own_segments[:, None] == ext_segments[None, :]
    doc_first = jnp.min(jnp.where(same_doc, column[None, :], ext_len), axis=1)
    positions = row_at - doc_first
    allowed = same_doc & (column[None, :] <= row_at[:, None])
    cosine, sine_table = rope_tables(positions)
    input_wide = hidden_in.astype(jnp.float32)
    gain_attn = gain_low.astype(jnp.float32)
    gain_mlp = mlp_low.astype(jnp.float32)
    normed_attn, inv_attn, scaled_attn = rms_forward(input_wide, gain_attn)
    attn_input = scaled_attn.astype(jnp.bfloat16)

    def all_rows(own, fetched):
        if shards == 2:
            other = ordered(fetched, swap(fetched, core_steps[0]), place, core_steps[0])
            return ordered(own, other, place, shard_steps[0])
        return lax.all_gather(own, "shard", axis=0, tiled=True)

    got_qkv = swap(qkv_half, shard_steps[0])
    got_qkv = after(got_qkv, cosine, sine_table, attn_input)
    full_qkv = all_rows(w_qkv, got_qkv)

    def columns_of(weight, owner):
        return lax.dynamic_slice_in_dim(weight, owner * ff_own + block_at, ff_block, 1)

    def block_rows(weight, earlier):
        own = columns_of(weight, shard)
        if shards == 2:
            got = swap(after(columns_of(weight, 1 - shard), earlier), shard_steps[0])
            return (ordered(own, got, place, shard_steps[0]), got)
        sent = jnp.stack([columns_of(weight, owner) for owner in range(shards)])
        got = lax.all_to_all(sent, "shard", split_axis=0, concat_axis=0, tiled=True)
        return (got.reshape(D, ff_block), got)

    out_half = pick(w_out.reshape(CORES, d_own // CORES, D), core)
    got_out = swap(after(out_half, got_qkv), shard_steps[0])
    full_out = all_rows(w_out, got_out)
    cot_rows = group_tokens(after(cotangent, got_qkv), group_steps)
    down_rows = lax.dynamic_slice_in_dim(w_down, block_at, ff_block, 0)
    once = block_at + jnp.arange(ff_block, dtype=jnp.int32) >= block * ff_block
    down_here = jnp.where(once[:, None], down_rows, jnp.zeros_like(down_rows))

    qkv_lin = jnp.dot(attn_input, full_qkv, preferred_element_type=jnp.float32) + bias_qkv
    rot = apply_rope(
        qkv_lin[:, : D + kv_width].reshape(tok_rows, HEADS + KV_HEADS, HEAD_DIM), cosine, sine_table
    ).astype(jnp.bfloat16)
    query_rot = rot[:, :HEADS]
    value_low = qkv_lin[:, D + kv_width :].astype(jnp.bfloat16)
    kv_ext = prior_rows(
        jnp.concatenate([rot[:, HEADS:].reshape(tok_rows, kv_width), value_low], axis=1),
        back_reach,
    )
    kv_ext = after(kv_ext, got_out)
    gate_here, got_gate = block_rows(w_gate, kv_ext)
    up_here, got_up = block_rows(w_up, kv_ext)
    keys_ext = kv_ext[:, :kv_width].reshape(ext_len, KV_HEADS, HEAD_DIM)
    values_ext = kv_ext[:, kv_width:].reshape(ext_len, KV_HEADS, HEAD_DIM)
    queries = query_rot.reshape(tok_rows, KV_HEADS, head_group, HEAD_DIM)
    scores = (
        jnp.einsum("qkgd,wkd->kgqw", queries, keys_ext, preferred_element_type=jnp.float32) * scale
    )
    scores = jnp.where(allowed[None, None], scores, MASKED)
    row_max = jnp.max(scores, axis=-1, keepdims=True)
    raw_weights = jnp.exp(scores - row_max)
    row_total = jnp.sum(raw_weights, axis=-1, keepdims=True)
    probs_low = (raw_weights / row_total).astype(jnp.bfloat16)
    log_total = row_max + jnp.log(row_total)
    attn_rows = jnp.einsum(
        "kgqw,wkd->qkgd", probs_low, values_ext, preferred_element_type=jnp.float32
    ).astype(jnp.bfloat16)
    attn_out = attn_rows.reshape(tok_rows, D)
    after_attn = input_wide + jnp.dot(attn_out, full_out, preferred_element_type=jnp.float32)
    normed_mlp, inv_mlp, scaled_mlp = rms_forward(after_attn, gain_mlp)
    mlp_input = scaled_mlp.astype(jnp.bfloat16)

    mlp_rows = group_tokens(mlp_input, group_steps)
    gate_lin = jnp.dot(mlp_rows, gate_here, preferred_element_type=jnp.float32)
    up_lin = jnp.dot(mlp_rows, up_here, preferred_element_type=jnp.float32)
    gate_sig = jax.nn.sigmoid(gate_lin)
    gate_act = gate_lin * gate_sig
    hidden_low = (gate_act * up_lin).astype(jnp.bfloat16)
    z_halves = (2,) * len(z_steps)
    grad_hidden = jnp.einsum("td,fd->tf", cot_rows, down_here, preferred_element_type=jnp.float32)
    grad_gate_lin = (grad_hidden * up_lin * gate_sig * (1.0 + gate_lin * (1.0 - gate_sig))).astype(
        jnp.bfloat16
    )
    grad_up_lin = (grad_hidden * gate_act).astype(jnp.bfloat16)
    by_tiles = (d_own // zs) % 16 == 0 and (ff_block // zs) % 16 == 0 and ff_own % 128 == 0
    if by_tiles:
        all_parts = weight_sums(
            mlp_rows, cot_rows, hidden_low, grad_gate_lin, grad_up_lin, zs, shards
        )
    else:
        down_parts = token_sum(hidden_low, cot_rows)
        gate_parts = token_sum(mlp_rows, grad_gate_lin)
        up_parts = token_sum(mlp_rows, grad_up_lin)
    normed_parts = jnp.einsum(
        "tf,df->td", grad_gate_lin, gate_here, preferred_element_type=jnp.float32
    ) + jnp.einsum(
        "tf,df->td",
        grad_up_lin,
        up_here,
        preferred_element_type=jnp.float32,
    )
    block_rows_out = D // zs
    tiles_in, tiles_out = D // 128, ff_block // 128

    def as_block(parts):
        parts = parts.reshape(zs, ff_block // zs, tiles_in, 128).transpose(0, 2, 1, 3)
        parts = parts.reshape(zs, tiles_out, block_rows_out, 128).transpose(0, 2, 1, 3)
        return parts.reshape(zs, block_rows_out, ff_block)

    def from_block(whole):
        lead = whole.shape[:-2]
        whole = whole.reshape(lead + (block_rows_out, tiles_out, 128)).swapaxes(-3, -2)
        whole = whole.reshape(lead + (tiles_in, ff_block // zs, 128)).swapaxes(-3, -2)
        return whole.reshape(lead + (ff_block // zs, D))

    def by_z(parts):
        parts = parts.reshape(shards, zs, d_own // zs, ff_block).swapaxes(0, 1)
        return parts.reshape(zs, block_rows_out, ff_block)

    if not by_tiles:
        all_parts = jnp.stack([as_block(down_parts), by_z(gate_parts), by_z(up_parts)], axis=1)
    same_yc = [[z * blocks + index for z in range(zs)] for index in range(blocks)]
    all_sum = lax.psum_scatter(
        all_parts, "rep", scatter_dimension=0, axis_index_groups=same_yc, tiled=False
    )
    grad_mlp_normed = group_sum(normed_parts, group_steps)

    def from_rep(piece):
        whole = lax.all_gather(piece, "rep", axis=0)
        return whole.reshape((zs, blocks) + piece.shape)

    grad_part, grad_mlp_gain = rms_backward(grad_mlp_normed, normed_mlp, inv_mlp, gain_mlp)
    grad_after = cotangent.astype(jnp.float32) + grad_part
    after_low = grad_after.astype(jnp.bfloat16)

    def half_sum(left, right):
        columns = left.reshape(tok_rows, shards, CORES, d_own // CORES)
        kept, sent = pick(columns, core, 2), pick(columns, 1 - core, 2)
        columns = jnp.concatenate([kept, swap(sent, core_steps[0])], axis=0)
        right = jnp.concatenate([right, swap(right, core_steps[0])], axis=0)
        return token_sum(columns.reshape(CORES * tok_rows, -1), right)

    def attn_scatter(parts):
        parts = parts.reshape((shards, -1, parts.shape[1]))
        if shards == 2:
            parts = scatter(parts, place, shard_steps)
        else:
            parts = lax.psum_scatter(parts, "shard", scatter_dimension=0)
        parts = scatter(parts.reshape(z_halves + (-1, parts.shape[1])), place, z_steps)
        for step in y_steps:
            got = swap(parts, step).astype(jnp.float32)
            parts = (parts.astype(jnp.float32) + got).astype(jnp.bfloat16)
        return parts

    out_sum = attn_scatter(half_sum(attn_out, after_low))
    grad_attn_out = jnp.einsum(
        "te,de->td", after_low, full_out, preferred_element_type=jnp.float32
    ).astype(jnp.bfloat16)
    grad_rows = grad_attn_out.reshape(tok_rows, KV_HEADS, head_group, HEAD_DIM)
    soft_probs = jnp.exp(scores - log_total)
    probs_back = soft_probs.astype(jnp.bfloat16)
    grad_values_ext = jnp.einsum(
        "kgqw,qkgd->wkd", probs_back, grad_rows, preferred_element_type=jnp.float32
    )
    grad_probs = jnp.einsum(
        "qkgd,wkd->kgqw", grad_rows, values_ext, preferred_element_type=jnp.float32
    )
    delta = jnp.sum(grad_rows.astype(jnp.float32) * attn_rows.astype(jnp.float32), axis=-1)
    delta = jnp.transpose(delta, (1, 2, 0))[..., None]
    grad_scores = (soft_probs * (grad_probs - delta) * scale).astype(jnp.bfloat16)
    grad_queries = jnp.einsum(
        "kgqw,wkd->qkgd", grad_scores, keys_ext, preferred_element_type=jnp.float32
    )
    grad_keys_ext = jnp.einsum(
        "kgqw,qkgd->wkd", grad_scores, queries, preferred_element_type=jnp.float32
    )
    grads_ext = jnp.concatenate(
        [grad_keys_ext.reshape(ext_len, kv_width), grad_values_ext.reshape(ext_len, kv_width)],
        axis=1,
    )
    grad_kv = return_rows(grads_ext, tok_rows, back_reach)
    in_sum = all_sum[1:].reshape(2, shards, d_own // zs, ff_block).swapaxes(0, 1)
    in_piece = exchange(in_sum, place, grads_ext).swapaxes(0, 1)
    all_piece = jnp.concatenate(
        [all_sum[:1], in_piece.reshape(2, block_rows_out, ff_block)], axis=0
    )
    all_all = from_rep(all_piece)
    out_parts = jnp.dot(
        after(hidden_low, grads_ext), down_here, preferred_element_type=jnp.float32
    )
    layer_out = after_attn + group_sum(out_parts, group_steps)
    grad_query_lin = undo_rope(
        grad_queries.reshape(tok_rows, HEADS, HEAD_DIM), cosine, sine_table
    ).reshape(tok_rows, D)
    grad_key_lin = undo_rope(
        grad_kv[:, :kv_width].reshape(tok_rows, KV_HEADS, HEAD_DIM), cosine, sine_table
    ).reshape(tok_rows, kv_width)
    grad_qkv = jnp.concatenate([grad_query_lin, grad_key_lin, grad_kv[:, kv_width:]], axis=1)
    grad_b_qkv = jnp.sum(grad_qkv, axis=0)
    qkv_low = grad_qkv.astype(jnp.bfloat16)
    grad_attn_normed = jnp.einsum(
        "te,de->td", qkv_low, full_qkv, preferred_element_type=jnp.float32
    )
    grad_front, grad_attn_gain = rms_backward(grad_attn_normed, normed_attn, inv_attn, gain_attn)
    grad_input = grad_after + grad_front

    query_parts = half_sum(attn_input, qkv_low)
    query_sum = attn_scatter(query_parts)
    piece = jnp.concatenate([query_sum, out_sum], axis=1)
    attn_half = piece
    for index, step in enumerate(z_steps[::-1]):
        mine = jnp.expand_dims(attn_half, index)
        got = jnp.expand_dims(swap(attn_half, step), index)
        attn_half = ordered(mine, got, place, step, index)
    attn_half = attn_half.reshape(-1, attn_half.shape[-1])
    attn_all = ordered(attn_half, swap(attn_half, core_steps[0]), place, core_steps[0])
    attn_all = attn_all.astype(jnp.float32)
    final_qkv, final_out = attn_all[:, :qkv_width], attn_all[:, qkv_width:]

    vectors = sum_everywhere(jnp.concatenate([grad_attn_gain, grad_b_qkv, grad_mlp_gain]))

    def own_part(first, count):
        return lax.dynamic_slice_in_dim(
            vectors, first + shard * (count // shards), count // shards, 0
        )

    if by_tiles:
        final_gate, final_up, final_down = weights_in_place(all_all, shards, ff_own)
    else:
        kept = [slice(kept_of(index, ff_block, ff_own)[1], ff_block) for index in range(blocks)]
        down_all = from_block(all_all[:, :, 0])
        in_all = all_all[:, :, 1:].reshape(zs, blocks, 2, shards, d_own // zs, ff_block)

        def in_place(pieces):
            columns = []
            for owner in range(shards):
                for index in range(blocks):
                    whole = pieces[:, index, owner].reshape(d_own, ff_block)
                    columns.append(whole[:, kept[index]])
            return jnp.concatenate(columns, axis=1).astype(jnp.float32)

        final_down = jnp.concatenate(
            [down_all[:, index].reshape(ff_block, D)[kept[index]] for index in range(blocks)], axis=0
        ).astype(jnp.float32)
        final_gate = in_place(in_all[:, :, 0])
        final_up = in_place(in_all[:, :, 1])
    return (
        layer_out,
        grad_input,
        own_part(0, D),
        final_qkv[:, :D],
        own_part(D, D),
        final_qkv[:, D : D + kv_width],
        own_part(2 * D, kv_width),
        final_qkv[:, D + kv_width :],
        own_part(2 * D + kv_width, kv_width),
        final_out,
        own_part(2 * D + 2 * kv_width, D),
        final_gate,
        final_up,
        final_down,
    )


def solution(mesh):
    return jax.shard_map(
        per_device,
        mesh=mesh,
        in_specs=(
            P(("rep", "shard"), None),
            P(("rep", "shard")),
            P("shard"),
            P("shard", None),
            P("shard"),
            P("shard", None),
            P("shard"),
            P("shard", None),
            P("shard"),
            P("shard", None),
            P("shard"),
            P("shard", None),
            P("shard", None),
            P("shard", None),
            P(("rep", "shard"), None),
        ),
        out_specs=(
            P(("rep", "shard"), None),
            P(("rep", "shard"), None),
            P("shard"),
            P("shard", None),
            P("shard"),
            P("shard", None),
            P("shard"),
            P("shard", None),
            P("shard"),
            P("shard", None),
            P("shard"),
            P("shard", None),
            P("shard", None),
            P("shard", None),
        ),
        check_vma=False,
    )
```

```python
import math

import jax
import jax.numpy as jnp
from jax import lax
from jax.experimental import pallas as pl
from jax.experimental.pallas import tpu as pltpu
from jax.sharding import PartitionSpec as P

D = 896
HEADS = 14
KV_HEADS = 2
HEAD_DIM = 64
SEQ = 512


EPSILON = 1e-06
ROPE_THETA = 1000000.0
MASKED = -1e30

CORES = 2
ALONG_Z = 4


def passed_along(shard, axis, by):
    peers = lax.axis_size(axis)
    pairs = [(i, i + by) for i in range(peers) if 0 <= i + by < peers]
    return lax.ppermute(shard, axis, pairs)


def rep_sizes():
    planes = lax.axis_size("rep") // CORES
    zs = min(ALONG_Z, planes)
    return (zs, planes // zs)


def own_place():
    zs, ys = rep_sizes()
    rep = lax.axis_index("rep")
    plane = rep // CORES
    return {"z": plane // ys, "y": plane % ys, "core": rep % CORES, "shard": lax.axis_index("shard")}


def steps_of(axis):
    zs, ys = rep_sizes()
    size = {"z": zs, "y": ys, "core": CORES, "shard": lax.axis_size("shard")}[axis]
    return [(axis, 1 << i) for i in range(size.bit_length() - 1)]


def swap(value, step):
    axis, bit = step
    if axis == "shard":
        peers = lax.axis_size("shard")
        return lax.ppermute(value, "shard", [(i, i ^ bit) for i in range(peers)])
    zs, ys = rep_sizes()
    pairs = []
    for rep in range(zs * ys * CORES):
        at = {"z": rep // CORES // ys, "y": rep // CORES % ys, "core": rep % CORES}
        at[axis] ^= bit
        pairs.append((rep, (at["z"] * ys + at["y"]) * CORES + at["core"]))
    return lax.ppermute(value, "rep", pairs)


def own_bit(place, step):
    return place[step[0]] // step[1] % 2


def nothing(*refs):
    pass


def after(value, *earlier):
    anywhere = pl.BlockSpec(memory_space=pl.ANY)
    return pl.pallas_call(
        nothing,
        out_shape=jax.ShapeDtypeStruct(value.shape, value.dtype),
        in_specs=[anywhere] * (1 + len(earlier)),
        out_specs=anywhere,
        input_output_aliases={0: 0},
        cost_estimate=pl.CostEstimate(flops=0, bytes_accessed=0, transcendentals=0),
        name="after",
    )(value, *earlier)


def pick(whole, at, axis=0):
    return lax.dynamic_index_in_dim(whole, at, axis, keepdims=False)


def ordered(mine, got, place, step, axis=0):
    first = own_bit(place, step) == 0
    return jnp.where(
        first, jnp.concatenate([mine, got], axis=axis), jnp.concatenate([got, mine], axis=axis)
    )


def gather(piece, place, steps):
    for step in steps:
        piece = ordered(piece, swap(piece, step), place, step)
    return piece


def scatter_step(parts, place, step, axis=0, earlier=()):
    at = own_bit(place, step)
    got = swap(pick(parts, 1 - at, axis), step)
    if earlier:
        got = after(got, *earlier)
    total = pick(parts, at, axis).astype(jnp.float32) + got.astype(jnp.float32)
    return total.astype(jnp.bfloat16)


def scatter(parts, place, steps, lead=0, earlier=()):
    for index, step in enumerate(steps):
        parts = scatter_step(
            parts, place, step, lead + len(steps) - 1 - index, earlier[index : index + 1]
        )
    return parts


def exchange(parts, place, earlier):
    shards = lax.axis_size("shard")
    if shards == 2:
        at = place["shard"]
        got = after(swap(pick(parts, 1 - at), ("shard", 1)), earlier)
        return ordered(pick(parts, at)[None], got[None], place, ("shard", 1))
    return lax.all_to_all(parts, "shard", split_axis=0, concat_axis=0, tiled=True)


def group_tokens(rows, steps):
    for step in steps:
        rows = jnp.concatenate([rows, swap(rows, step)], axis=0)
    return rows


def group_step(parts, step, earlier=()):
    half = parts.shape[0] // 2
    sent = parts[half:]
    if step[0] != "core":
        sent = sent.astype(jnp.bfloat16)
    got = swap(sent, step)
    if earlier:
        got = after(got, *earlier)
    return parts[:half] + got.astype(jnp.float32)


def group_sum(parts, steps):
    for step in steps[::-1]:
        parts = group_step(parts, step)
    return parts


def rope_tables(positions):
    half_width = HEAD_DIM // 2
    inverse = ROPE_THETA ** (-(jnp.arange(half_width, dtype=jnp.float32) * 2.0) / HEAD_DIM)
    angle_half = positions.astype(jnp.float32)[:, None] * inverse[None, :]
    angle_full = jnp.concatenate([angle_half, angle_half], axis=-1)
    return (jnp.cos(angle_full), jnp.sin(angle_full))


def rotate_half(values):
    half_width = values.shape[-1] // 2
    return jnp.concatenate([-values[..., half_width:], values[..., :half_width]], axis=-1)


def rotate_back(values):
    half_width = values.shape[-1] // 2
    return jnp.concatenate([values[..., half_width:], -values[..., :half_width]], axis=-1)


def apply_rope(values, cosine, sine_table):
    return values * cosine[:, None, :] + rotate_half(values) * sine_table[:, None, :]


def undo_rope(grads, cosine, sine_table):
    return grads * cosine[:, None, :] + rotate_back(grads * sine_table[:, None, :])


def rms_forward(values, gain):
    inv_scale = lax.rsqrt(jnp.mean(values * values, axis=-1, keepdims=True) + EPSILON)
    normed = values * inv_scale
    return (normed, inv_scale, normed * gain)


def rms_backward(grads, normed, inv_scale, gain):
    through = grads * gain
    inner = jnp.mean(through * normed, axis=-1, keepdims=True)
    return (inv_scale * (through - normed * inner), jnp.sum(grads * normed, axis=0))


def spans(first, count, size):
    cuts = []
    at = first
    while at < first + count:
        end = min((at // size + 1) * size, first + count)
        cuts.append((at // size, at % size, at - first, end - at))
        at = end
    return cuts


def kept_of(index, ff_block, ff_own):
    at = min(index * ff_block, ff_own - ff_block)
    return (at, min(index * ff_block - at, ff_block))


def weight_sums(mlp_rows, cot_rows, hidden_low, grad_gate, grad_up, zs, shards):
    tokens, width = mlp_rows.shape
    units = hidden_low.shape[1]
    rows = width // zs
    d_z = width // shards // zs
    f_z = units // zs

    def kernel(x_ref, cot_ref, hidden_ref, gate_ref, up_ref, out_ref):
        def chunks(size):
            return [(at, min(256, size - at)) for at in range(0, size, 256)]

        def column_sum(left, right_ref):
            got = jnp.dot(left, right_ref[...], preferred_element_type=jnp.float32)
            return got.astype(jnp.bfloat16)

        for first, wide in chunks(units):
            got = column_sum(hidden_ref[:, first : first + wide].T, cot_ref)
            for z, row, at, count in spans(first, wide, f_z):
                for tile in range(width // 128):
                    piece = got[at : at + count, tile * 128 : (tile + 1) * 128]
                    for to, to_row, from_row, length in spans(tile * f_z + row, count, rows):
                        out_ref[z, 0, to_row : to_row + length, to * 128 : (to + 1) * 128] = piece[
                            from_row : from_row + length
                        ]
        for first, wide in chunks(width):
            left = x_ref[:, first : first + wide].T
            for index, right_ref in ((1, gate_ref), (2, up_ref)):
                got = column_sum(left, right_ref)
                for part, row, at, count in spans(first, wide, d_z):
                    to_row = part // zs * d_z + row
                    out_ref[part % zs, index, to_row : to_row + count] = got[at : at + count]

    operands = (mlp_rows, cot_rows, hidden_low, grad_gate, grad_up)
    return pl.pallas_call(
        kernel,
        out_shape=jax.ShapeDtypeStruct((zs, 3, rows, units), jnp.bfloat16),
        in_specs=[pl.BlockSpec(memory_space=pltpu.VMEM)] * 5,
        out_specs=pl.BlockSpec(memory_space=pltpu.VMEM),
        compiler_params=pltpu.CompilerParams(vmem_limit_bytes=48 * 1024 * 1024),
        cost_estimate=pl.CostEstimate(
            flops=6 * tokens * width * units, bytes_accessed=12 * 1024 * 1024, transcendentals=0
        ),
        name="weight_sums",
    )(*operands)


def weights_in_place(all_all, shards, ff_own):
    zs, blocks, _, rows, units = all_all.shape
    width = rows * zs
    d_z = rows // shards
    f_z = units // zs

    def kernel(all_ref, gate_ref, up_ref, down_ref, wide_ref, sems):
        z = pl.program_id(0)
        for index in range(blocks):
            for tile in range(width // 128):
                for part, row, at, count in spans(tile * f_z, f_z, rows):
                    wide_ref[index, at : at + count, tile * 128 : (tile + 1) * 128] = all_ref[
                        0, index, 0, row : row + count, part * 128 : (part + 1) * 128
                    ].astype(jnp.float32)

        def move(index, skip):
            at = kept_of(index, units, ff_own)[0]
            to = pl.multiple_of(at + z * f_z + skip, 8)
            return pltpu.make_async_copy(
                wide_ref.at[index, pl.ds(skip, f_z - skip)],
                down_ref.at[pl.ds(to, f_z - skip)],
                sems.at[index],
            )

        def each_move(act):
            for index in range(blocks):
                dropped = kept_of(index, units, ff_own)[1]
                for place in range(zs):
                    skip = min(max(dropped - place * f_z, 0), f_z)
                    if skip < f_z:

                        @pl.when(z == place)
                        def _(index=index, skip=skip):
                            act(move(index, skip))

        each_move(lambda copy: copy.start())
        for number, out_ref in ((1, gate_ref), (2, up_ref)):
            for owner in range(shards):
                for index in range(blocks):
                    at, skip = kept_of(index, units, ff_own)
                    if skip < units:
                        out_ref[:, owner * ff_own + at + skip : owner * ff_own + at + units] = all_ref[
                            0, index, number, owner * d_z : (owner + 1) * d_z, skip:
                        ].astype(jnp.float32)
        each_move(lambda copy: copy.wait())

    wide = jax.ShapeDtypeStruct((d_z * zs, shards * ff_own), jnp.float32)
    return pl.pallas_call(
        kernel,
        grid=(zs,),
        out_shape=(wide, wide, jax.ShapeDtypeStruct((ff_own, width), jnp.float32)),
        in_specs=[pl.BlockSpec((1, blocks, 3, rows, units), lambda z: (z, 0, 0, 0, 0))],
        out_specs=(
            pl.BlockSpec((d_z, shards * ff_own), lambda z: (z, 0)),
            pl.BlockSpec((d_z, shards * ff_own), lambda z: (z, 0)),
            pl.BlockSpec(memory_space=pl.ANY),
        ),
        scratch_shapes=[
            pltpu.VMEM((blocks, f_z, width), jnp.float32),
            pltpu.SemaphoreType.DMA((blocks,)),
        ],
        compiler_params=pltpu.CompilerParams(vmem_limit_bytes=48 * 1024 * 1024),
        cost_estimate=pl.CostEstimate(flops=0, bytes_accessed=44 * 1024 * 1024, transcendentals=0),
        name="weights_in_place",
    )(all_all)


def prior_rows(rows, back_reach):
    parts = []
    for distance in range(back_reach, 0, -1):
        parts.append(passed_along(rows, ("rep", "shard"), distance))
    parts.append(rows)
    return jnp.concatenate(parts, axis=0)


def return_rows(grads, tok_rows, back_reach):
    total = grads[back_reach * tok_rows :]
    for distance in range(back_reach, 0, -1):
        first_row = (back_reach - distance) * tok_rows
        total = total + passed_along(
            grads[first_row : first_row + tok_rows], ("rep", "shard"), -distance
        )
    return total


def token_sum(left, right):
    return lax.dot_general(
        left, right, (((0,), (0,)), ((), ())), preferred_element_type=jnp.float32
    ).astype(jnp.bfloat16)


def per_device(
    hidden_in,
    segments,
    attn_gain,
    w_query,
    b_query,
    w_key,
    b_key,
    w_value,
    b_value,
    w_out,
    mlp_gain,
    w_gate,
    w_up,
    w_down,
    cotangent,
):
    tok_rows = hidden_in.shape[0]
    back_reach = (SEQ - 2) // tok_rows + 1
    head_group = HEADS // KV_HEADS
    kv_width = KV_HEADS * HEAD_DIM
    qkv_width = D + 2 * kv_width
    scale = 1.0 / math.sqrt(HEAD_DIM)
    place = own_place()
    core, shard = place["core"], place["shard"]
    shards = lax.axis_size("shard")
    zs, ys = rep_sizes()
    d_own = D // shards
    shard_steps, y_steps, z_steps, core_steps = [
        steps_of(axis) for axis in ("shard", "y", "z", "core")
    ]
    group_steps = shard_steps + y_steps + core_steps

    ff_own = w_down.shape[0]
    blocks = ys * CORES
    ff_block = min(ff_own, -(-ff_own // (blocks * 128)) * 128)
    block = place["y"] * CORES + core
    block_at = jnp.minimum(block * ff_block, ff_own - ff_block)

    w_qkv = jnp.concatenate([w_query, w_key, w_value], axis=1)
    qkv_half = pick(w_qkv.reshape(CORES, d_own // CORES, qkv_width), core)
    small = jnp.concatenate([attn_gain, b_query, b_key, b_value, mlp_gain])
    own_segments = segments + 1
    group_is_reach = shards == 2 and CORES * shards == back_reach
    window_at = (core * shards + shard) * tok_rows

    def window(rows):
        rows = rows.reshape((2 * back_reach * tok_rows,) + rows.shape[4:])
        return lax.dynamic_slice_in_dim(rows, window_at, (back_reach + 1) * tok_rows, 0)

    def as_rows(vector, count):
        return jnp.pad(vector, (0, count * qkv_width - vector.shape[0])).reshape(count, qkv_width)

    def columns_of(weight, owner):
        return lax.dynamic_slice_in_dim(weight, owner * ff_own + block_at, ff_block, 1)

    columns_sent = [
        pick(
            columns_of(weight, (shard + 1) % shards).reshape(2, d_own // 2, ff_block),
            own_bit(place, z_steps[0]),
        )
        for weight in (w_gate, w_up)
    ]
    if group_is_reach:
        far = passed_along(own_segments, ("rep", "shard"), back_reach)
        both = jnp.concatenate([far, own_segments]).astype(jnp.bfloat16)
        extra = -(-(small.shape[0] + 2 * tok_rows) // (16 * qkv_width)) * 16
        sent = as_rows(jnp.concatenate([small, both]), extra)
        got = swap(jnp.concatenate([qkv_half, sent], axis=0), shard_steps[0])
        got = after(got, *columns_sent)
        got_qkv, got_small = got[:-extra], got[-extra:].reshape(-1)
        small_all = ordered(small[None], got_small[None, : small.shape[0]], place, shard_steps[0])
        got_both = got_small[small.shape[0] : small.shape[0] + 2 * tok_rows]
        both = ordered(
            both.reshape(2, 1, tok_rows), got_both.reshape(2, 1, tok_rows), place, shard_steps[0], 1
        )
        sent = as_rows(both.reshape(-1), 16)
        other_qkv = swap(jnp.concatenate([got_qkv, sent], axis=0), core_steps[0])
        got_both = other_qkv[-16:].reshape(-1)[: both.size].reshape(2, 1, shards, tok_rows)
        both = ordered(both[:, None], got_both, place, core_steps[0], 1)
        ext_segments = window(both.reshape(both.shape)).astype(jnp.int32)
        other_qkv = ordered(got_qkv, other_qkv[:-16], place, core_steps[0])
        full_qkv = ordered(w_qkv, other_qkv, place, shard_steps[0])
    else:
        small_all = gather(small[None], place, shard_steps)
        ext_segments = prior_rows(own_segments, back_reach)
        got_qkv = w_qkv
        full_qkv = lax.all_gather(w_qkv, "shard", axis=0, tiled=True)
    kv_own = kv_width // shards
    cuts = [0, d_own, 2 * d_own, 2 * d_own + kv_own, 2 * d_own + 2 * kv_own, small.shape[0]]
    gain_low, bias_query, bias_key, bias_value, mlp_low = [
        small_all[:, a:b].reshape(-1) for a, b in zip(cuts[:-1], cuts[1:])
    ]
    bias_qkv = jnp.concatenate([bias_query, bias_key, bias_value]).astype(jnp.float32)

    ext_len = ext_segments.shape[0]
    column = jnp.arange(ext_len, dtype=jnp.int32)
    row_at = back_reach * tok_rows + jnp.arange(tok_rows, dtype=jnp.int32)
    same_doc = own_segments[:, None] == ext_segments[None, :]
    doc_first = jnp.min(jnp.where(same_doc, column[None, :], ext_len), axis=1)
    positions = row_at - doc_first
    allowed = same_doc & (column[None, :] <= row_at[:, None])
    cosine, sine_table = rope_tables(positions)
    input_wide = hidden_in.astype(jnp.float32)
    gain_attn = gain_low.astype(jnp.float32)
    gain_mlp = mlp_low.astype(jnp.float32)
    normed_attn, inv_attn, scaled_attn = rms_forward(input_wide, gain_attn)
    attn_input = scaled_attn.astype(jnp.bfloat16)

    def all_rows(own, fetched):
        if shards == 2:
            for step in y_steps:
                fetched = ordered(fetched, swap(fetched, step), place, step)
            other = ordered(fetched, swap(fetched, core_steps[0]), place, core_steps[0])
            return ordered(own, other, place, shard_steps[0])
        return lax.all_gather(own, "shard", axis=0, tiled=True)


    def block_rows(weight, sent, earlier):
        own = columns_of(weight, shard)
        if shards == 2:
            got = swap(after(sent, earlier), shard_steps[0])
            other = ordered(got, swap(got, z_steps[0]), place, z_steps[0])
            return (ordered(own, other, place, shard_steps[0]), got, other)
        sent = jnp.stack([columns_of(weight, owner) for owner in range(shards)])
        got = lax.all_to_all(sent, "shard", split_axis=0, concat_axis=0, tiled=True)
        return (got.reshape(D, ff_block), got, got)

    out_part = pick(w_out.reshape(CORES, ys, d_own // CORES // ys, D), core)
    out_part = pick(out_part, place["y"])
    got_out = swap(after(out_part, got_qkv), shard_steps[0])
    cot_shards = group_tokens(after(cotangent, got_qkv), shard_steps)
    cot_ys = group_tokens(cot_shards, y_steps)
    cot_rows = group_tokens(cot_ys, core_steps)
    gate_here, got_gate, other_gate = block_rows(w_gate, columns_sent[0], got_qkv)
    up_here, got_up, other_up = block_rows(w_up, columns_sent[1], got_qkv)
    down_rows = lax.dynamic_slice_in_dim(w_down, block_at, ff_block, 0)
    once = block_at + jnp.arange(ff_block, dtype=jnp.int32) >= block * ff_block
    down_here = jnp.where(once[:, None], down_rows, jnp.zeros_like(down_rows))

    qkv_lin = jnp.dot(attn_input, full_qkv, preferred_element_type=jnp.float32) + bias_qkv
    rot = apply_rope(
        qkv_lin[:, : D + kv_width].reshape(tok_rows, HEADS + KV_HEADS, HEAD_DIM), cosine, sine_table
    ).astype(jnp.bfloat16)
    query_rot = rot[:, :HEADS]
    value_low = qkv_lin[:, D + kv_width :].astype(jnp.bfloat16)
    kv_own_rows = jnp.concatenate([rot[:, HEADS:].reshape(tok_rows, kv_width), value_low], axis=1)
    if group_is_reach:
        far = passed_along(kv_own_rows, ("rep", "shard"), back_reach)
        both = after(jnp.stack([far, kv_own_rows])[:, None], got_gate)
        both = ordered(both, swap(both, shard_steps[0]), place, shard_steps[0], 1)[:, None]
        both = ordered(both, swap(both, core_steps[0]), place, core_steps[0], 1)
        kv_ext = window(both)
    else:
        kv_ext = prior_rows(kv_own_rows, back_reach)
    full_out = all_rows(w_out, after(got_out, kv_own_rows))
    kv_ext = after(kv_ext, got_up, cot_shards)
    keys_ext = kv_ext[:, :kv_width].reshape(ext_len, KV_HEADS, HEAD_DIM)
    values_ext = kv_ext[:, kv_width:].reshape(ext_len, KV_HEADS, HEAD_DIM)
    queries = query_rot.reshape(tok_rows, KV_HEADS, head_group, HEAD_DIM)
    scores = (
        jnp.einsum("qkgd,wkd->kgqw", queries, keys_ext, preferred_element_type=jnp.float32) * scale
    )
    scores = jnp.where(allowed[None, None], scores, MASKED)
    row_max = jnp.max(scores, axis=-1, keepdims=True)
    raw_weights = jnp.exp(scores - row_max)
    row_total = jnp.sum(raw_weights, axis=-1, keepdims=True)
    probs_low = (raw_weights / row_total).astype(jnp.bfloat16)
    log_total = row_max + jnp.log(row_total)
    attn_rows = jnp.einsum(
        "kgqw,wkd->qkgd", probs_low, values_ext, preferred_element_type=jnp.float32
    ).astype(jnp.bfloat16)
    attn_out = attn_rows.reshape(tok_rows, D)
    after_attn = input_wide + jnp.dot(attn_out, full_out, preferred_element_type=jnp.float32)
    normed_mlp, inv_mlp, scaled_mlp = rms_forward(after_attn, gain_mlp)
    mlp_input = after(scaled_mlp.astype(jnp.bfloat16), other_gate, cot_ys)

    mlp_rows = group_tokens(mlp_input, shard_steps)
    mlp_rows = group_tokens(after(mlp_rows, other_up), y_steps + core_steps)
    gate_lin = jnp.dot(mlp_rows, gate_here, preferred_element_type=jnp.float32)
    up_lin = jnp.dot(mlp_rows, up_here, preferred_element_type=jnp.float32)
    gate_sig = jax.nn.sigmoid(gate_lin)
    gate_act = gate_lin * gate_sig
    hidden_low = (gate_act * up_lin).astype(jnp.bfloat16)
    z_halves = (2,) * len(z_steps)
    grad_hidden = jnp.einsum("td,fd->tf", cot_rows, down_here, preferred_element_type=jnp.float32)
    grad_gate_lin = (grad_hidden * up_lin * gate_sig * (1.0 + gate_lin * (1.0 - gate_sig))).astype(
        jnp.bfloat16
    )
    grad_up_lin = (grad_hidden * gate_act).astype(jnp.bfloat16)
    by_tiles = (d_own // zs) % 16 == 0 and (ff_block // zs) % 16 == 0 and ff_own % 128 == 0
    if by_tiles:
        all_parts = weight_sums(
            mlp_rows, cot_rows, hidden_low, grad_gate_lin, grad_up_lin, zs, shards
        )
    else:
        down_parts = token_sum(hidden_low, cot_rows)
        gate_parts = token_sum(mlp_rows, grad_gate_lin)
        up_parts = token_sum(mlp_rows, grad_up_lin)
    normed_parts = jnp.einsum(
        "tf,df->td", grad_gate_lin, gate_here, preferred_element_type=jnp.float32
    ) + jnp.einsum(
        "tf,df->td",
        grad_up_lin,
        up_here,
        preferred_element_type=jnp.float32,
    )
    block_rows_out = D // zs
    tiles_in, tiles_out = D // 128, ff_block // 128

    def as_block(parts):
        parts = parts.reshape(zs, ff_block // zs, tiles_in, 128).transpose(0, 2, 1, 3)
        parts = parts.reshape(zs, tiles_out, block_rows_out, 128).transpose(0, 2, 1, 3)
        return parts.reshape(zs, block_rows_out, ff_block)

    def from_block(whole):
        lead = whole.shape[:-2]
        whole = whole.reshape(lead + (block_rows_out, tiles_out, 128)).swapaxes(-3, -2)
        whole = whole.reshape(lead + (tiles_in, ff_block // zs, 128)).swapaxes(-3, -2)
        return whole.reshape(lead + (ff_block // zs, D))

    def by_z(parts):
        parts = parts.reshape(shards, zs, d_own // zs, ff_block).swapaxes(0, 1)
        return parts.reshape(zs, block_rows_out, ff_block)

    if not by_tiles:
        all_parts = jnp.stack([as_block(down_parts), by_z(gate_parts), by_z(up_parts)], axis=1)
    same_yc = [[z * blocks + index for z in range(zs)] for index in range(blocks)]
    all_sum = lax.psum_scatter(
        all_parts, "rep", scatter_dimension=0, axis_index_groups=same_yc, tiled=False
    )
    grad_mlp_normed = group_sum(normed_parts, group_steps)

    def from_rep(piece):
        whole = lax.all_gather(piece, "rep", axis=0)
        return whole.reshape((zs, blocks) + piece.shape)

    grad_part, grad_mlp_gain = rms_backward(grad_mlp_normed, normed_mlp, inv_mlp, gain_mlp)
    grad_after = cotangent.astype(jnp.float32) + grad_part
    after_low = grad_after.astype(jnp.bfloat16)
    out_parts = jnp.dot(
        after(hidden_low, after_low), down_here, preferred_element_type=jnp.float32
    )
    out_sums = group_sum(out_parts, y_steps + core_steps)

    def half_sum(left, right):
        columns = left.reshape(tok_rows, shards, CORES, d_own // CORES)
        kept, sent = pick(columns, core, 2), pick(columns, 1 - core, 2)
        columns = jnp.concatenate([kept, swap(sent, core_steps[0])], axis=0)
        right = jnp.concatenate([right, swap(right, core_steps[0])], axis=0)
        return token_sum(columns.reshape(CORES * tok_rows, -1), right)

    def shard_scatter(parts):
        parts = parts.reshape((shards, -1, parts.shape[1]))
        if shards == 2:
            return scatter(parts, place, shard_steps)
        return lax.psum_scatter(parts, "shard", scatter_dimension=0)

    out_sum = shard_scatter(half_sum(attn_out, after_low))
    grad_attn_out = jnp.einsum(
        "te,de->td", after_low, full_out, preferred_element_type=jnp.float32
    ).astype(jnp.bfloat16)
    grad_rows = grad_attn_out.reshape(tok_rows, KV_HEADS, head_group, HEAD_DIM)
    soft_probs = jnp.exp(scores - log_total)
    probs_back = soft_probs.astype(jnp.bfloat16)
    grad_values_ext = jnp.einsum(
        "kgqw,qkgd->wkd", probs_back, grad_rows, preferred_element_type=jnp.float32
    )
    grad_probs = jnp.einsum(
        "qkgd,wkd->kgqw", grad_rows, values_ext, preferred_element_type=jnp.float32
    )
    delta = jnp.sum(grad_rows.astype(jnp.float32) * attn_rows.astype(jnp.float32), axis=-1)
    delta = jnp.transpose(delta, (1, 2, 0))[..., None]
    grad_scores = (soft_probs * (grad_probs - delta) * scale).astype(jnp.bfloat16)
    grad_queries = jnp.einsum(
        "kgqw,wkd->qkgd", grad_scores, keys_ext, preferred_element_type=jnp.float32
    )
    grad_keys_ext = jnp.einsum(
        "kgqw,qkgd->wkd", grad_scores, queries, preferred_element_type=jnp.float32
    )
    grads_ext = jnp.concatenate(
        [grad_keys_ext.reshape(ext_len, kv_width), grad_values_ext.reshape(ext_len, kv_width)],
        axis=1,
    )
    grads_ext = after(grads_ext, out_sum, out_sums)
    layer_out = after_attn + group_sum(out_sums, shard_steps)
    grad_kv = return_rows(grads_ext, tok_rows, back_reach)
    in_sum = all_sum[1:].reshape(2, shards, d_own // zs, ff_block).swapaxes(0, 1)
    in_piece = exchange(in_sum, place, grads_ext).swapaxes(0, 1)
    all_piece = jnp.concatenate(
        [all_sum[:1], in_piece.reshape(2, block_rows_out, ff_block)], axis=0
    )
    all_all = from_rep(all_piece)
    grad_query_lin = undo_rope(
        grad_queries.reshape(tok_rows, HEADS, HEAD_DIM), cosine, sine_table
    ).reshape(tok_rows, D)
    grad_key_lin = undo_rope(
        grad_kv[:, :kv_width].reshape(tok_rows, KV_HEADS, HEAD_DIM), cosine, sine_table
    ).reshape(tok_rows, kv_width)
    grad_qkv = jnp.concatenate([grad_query_lin, grad_key_lin, grad_kv[:, kv_width:]], axis=1)
    grad_b_qkv = jnp.sum(grad_qkv, axis=0)
    qkv_low = after(grad_qkv.astype(jnp.bfloat16), layer_out)
    grad_attn_normed = jnp.einsum(
        "te,de->td", qkv_low, full_qkv, preferred_element_type=jnp.float32
    )
    grad_front, grad_attn_gain = rms_backward(grad_attn_normed, normed_attn, inv_attn, gain_attn)
    grad_input = grad_after + grad_front

    vectors = jnp.concatenate([grad_attn_gain, grad_b_qkv, grad_mlp_gain])
    vectors = vectors + swap(vectors, core_steps[0])
    ends = [0, D, 2 * D, 2 * D + kv_width, qkv_width + D, qkv_width + 2 * D]
    vectors = jnp.concatenate(
        [vectors[a:b].reshape(shards, -1) for a, b in zip(ends[:-1], ends[1:])], axis=1
    )
    vectors = pick(vectors.reshape(shards, CORES, zs, 1, -1), core, 1).astype(jnp.bfloat16)
    vector_len = vectors.shape[-1]
    piece_rows = d_own // CORES // zs
    below = 16 - piece_rows % 16
    vectors = jnp.pad(vectors, ((0, 0), (0, 0), (0, below - 1), (0, qkv_width - vector_len)))
    query_parts = half_sum(attn_input, qkv_low).reshape(shards, zs, piece_rows, qkv_width)
    query_parts = jnp.concatenate([query_parts, vectors], axis=2)
    query_sum = shard_scatter(query_parts.reshape(-1, qkv_width))
    out_sum = out_sum.reshape(zs, piece_rows, D)
    out_sum = jnp.pad(out_sum, ((0, 0), (0, below), (0, 0))).reshape(-1, D)
    parts = jnp.concatenate([query_sum.reshape(-1, qkv_width), out_sum], axis=1)
    y_halves = (2,) * len(y_steps)
    parts = scatter(parts.reshape(parts.shape[:1] + y_halves + (-1,)), place, y_steps, 1)
    piece = scatter(parts.reshape(z_halves + (-1, parts.shape[1])), place, z_steps)
    for index, step in enumerate(y_steps[::-1]):
        mine = jnp.expand_dims(piece, index + 1)
        got = jnp.expand_dims(swap(piece, step), index + 1)
        piece = ordered(mine, got, place, step, index + 1)
    piece = piece.reshape(piece.shape[0], -1)
    if by_tiles:
        final_gate, final_up, final_down = weights_in_place(all_all, shards, ff_own)
    attn_half = piece
    for index, step in enumerate(z_steps[::-1]):
        mine = jnp.expand_dims(attn_half, index)
        got = jnp.expand_dims(swap(attn_half, step), index)
        if by_tiles and index == len(z_steps) - 1:
            got = after(got, final_down)
        attn_half = ordered(mine, got, place, step, index)
    attn_half = attn_half.reshape(-1, attn_half.shape[-1])
    attn_other = swap(attn_half, core_steps[0])
    attn_all = ordered(attn_half, attn_other, place, core_steps[0])
    attn_all = attn_all.reshape(CORES * zs, piece_rows + below, qkv_width + D)
    vector_own = attn_all[:, piece_rows, :vector_len].reshape(-1).astype(jnp.float32)
    attn_all = attn_all[:, :piece_rows].reshape(d_own, qkv_width + D)
    edges = [0, D, D + kv_width, qkv_width, qkv_width + D]
    final_query, final_key, final_value, final_out = [
        attn_all[:, a:b].astype(jnp.float32) for a, b in zip(edges[:-1], edges[1:])
    ]
    final_gain, final_bq, final_bk, final_bv, final_mlp_gain = [
        vector_own[a:b] for a, b in zip(cuts[:-1], cuts[1:])
    ]

    if not by_tiles:
        kept = [slice(kept_of(index, ff_block, ff_own)[1], ff_block) for index in range(blocks)]
        down_all = from_block(all_all[:, :, 0])
        in_all = all_all[:, :, 1:].reshape(zs, blocks, 2, shards, d_own // zs, ff_block)

        def in_place(pieces):
            columns = []
            for owner in range(shards):
                for index in range(blocks):
                    whole = pieces[:, index, owner].reshape(d_own, ff_block)
                    columns.append(whole[:, kept[index]])
            return jnp.concatenate(columns, axis=1).astype(jnp.float32)

        final_down = jnp.concatenate(
            [down_all[:, index].reshape(ff_block, D)[kept[index]] for index in range(blocks)], axis=0
        ).astype(jnp.float32)
        final_gate = in_place(in_all[:, :, 0])
        final_up = in_place(in_all[:, :, 1])
    return (
        layer_out,
        grad_input,
        final_gain,
        final_query,
        final_bq,
        final_key,
        final_bk,
        final_value,
        final_bv,
        final_out,
        final_mlp_gain,
        final_gate,
        final_up,
        final_down,
    )


def solution(mesh):
    return jax.shard_map(
        per_device,
        mesh=mesh,
        in_specs=(
            P(("rep", "shard"), None),
            P(("rep", "shard")),
            P("shard"),
            P("shard", None),
            P("shard"),
            P("shard", None),
            P("shard"),
            P("shard", None),
            P("shard"),
            P("shard", None),
            P("shard"),
            P("shard", None),
            P("shard", None),
            P("shard", None),
            P(("rep", "shard"), None),
        ),
        out_specs=(
            P(("rep", "shard"), None),
            P(("rep", "shard"), None),
            P("shard"),
            P("shard", None),
            P("shard"),
            P("shard", None),
            P("shard"),
            P("shard", None),
            P("shard"),
            P("shard", None),
            P("shard"),
            P("shard", None),
            P("shard", None),
            P("shard", None),
        ),
        check_vma=False,
    )
```

```python
import math

import jax
import jax.numpy as jnp
from jax import lax
from jax.experimental import pallas as pl
from jax.experimental.pallas import tpu as pltpu
from jax.sharding import PartitionSpec as P

D = 896
HEADS = 14
KV_HEADS = 2
HEAD_DIM = 64
SEQ = 512


EPSILON = 1e-06
ROPE_THETA = 1000000.0
MASKED = -1e30

CORES = 2
ALONG_Z = 4


def passed_along(shard, axis, by):
    peers = lax.axis_size(axis)
    pairs = [(i, i + by) for i in range(peers) if 0 <= i + by < peers]
    return lax.ppermute(shard, axis, pairs)


def rep_sizes():
    planes = lax.axis_size("rep") // CORES
    zs = min(ALONG_Z, planes)
    return (zs, planes // zs)


def own_place():
    zs, ys = rep_sizes()
    rep = lax.axis_index("rep")
    plane = rep // CORES
    return {"z": plane // ys, "y": plane % ys, "core": rep % CORES, "shard": lax.axis_index("shard")}


def steps_of(axis):
    zs, ys = rep_sizes()
    size = {"z": zs, "y": ys, "core": CORES, "shard": lax.axis_size("shard")}[axis]
    return [(axis, 1 << i) for i in range(size.bit_length() - 1)]


def swap(value, step):
    axis, bit = step
    if axis == "shard":
        peers = lax.axis_size("shard")
        return lax.ppermute(value, "shard", [(i, i ^ bit) for i in range(peers)])
    zs, ys = rep_sizes()
    pairs = []
    for rep in range(zs * ys * CORES):
        at = {"z": rep // CORES // ys, "y": rep // CORES % ys, "core": rep % CORES}
        at[axis] ^= bit
        pairs.append((rep, (at["z"] * ys + at["y"]) * CORES + at["core"]))
    return lax.ppermute(value, "rep", pairs)


def own_bit(place, step):
    return place[step[0]] // step[1] % 2


def nothing(*refs):
    pass


def after(value, *earlier):
    anywhere = pl.BlockSpec(memory_space=pl.ANY)
    return pl.pallas_call(
        nothing,
        out_shape=jax.ShapeDtypeStruct(value.shape, value.dtype),
        in_specs=[anywhere] * (1 + len(earlier)),
        out_specs=anywhere,
        input_output_aliases={0: 0},
        cost_estimate=pl.CostEstimate(flops=0, bytes_accessed=0, transcendentals=0),
        name="after",
    )(value, *earlier)


def pick(whole, at, axis=0):
    return lax.dynamic_index_in_dim(whole, at, axis, keepdims=False)


def ordered(mine, got, place, step, axis=0):
    first = own_bit(place, step) == 0
    return jnp.where(
        first, jnp.concatenate([mine, got], axis=axis), jnp.concatenate([got, mine], axis=axis)
    )


def gather(piece, place, steps):
    for step in steps:
        piece = ordered(piece, swap(piece, step), place, step)
    return piece


def scatter_step(parts, place, step, axis=0, earlier=()):
    at = own_bit(place, step)
    got = swap(pick(parts, 1 - at, axis), step)
    if earlier:
        got = after(got, *earlier)
    total = pick(parts, at, axis).astype(jnp.float32) + got.astype(jnp.float32)
    return total.astype(jnp.bfloat16)


def scatter(parts, place, steps, lead=0, earlier=()):
    for index, step in enumerate(steps):
        parts = scatter_step(
            parts, place, step, lead + len(steps) - 1 - index, earlier[index : index + 1]
        )
    return parts


def exchange(parts, place, earlier):
    shards = lax.axis_size("shard")
    if shards == 2:
        at = place["shard"]
        got = after(swap(pick(parts, 1 - at), ("shard", 1)), earlier)
        return ordered(pick(parts, at)[None], got[None], place, ("shard", 1))
    return lax.all_to_all(parts, "shard", split_axis=0, concat_axis=0, tiled=True)


def group_tokens(rows, steps):
    for step in steps:
        rows = jnp.concatenate([rows, swap(rows, step)], axis=0)
    return rows


def group_step(parts, step, earlier=()):
    half = parts.shape[0] // 2
    sent = parts[half:]
    if step[0] != "core":
        sent = sent.astype(jnp.bfloat16)
    got = swap(sent, step)
    if earlier:
        got = after(got, *earlier)
    return parts[:half] + got.astype(jnp.float32)


def group_sum(parts, steps):
    for step in steps[::-1]:
        parts = group_step(parts, step)
    return parts


def rope_tables(positions):
    half_width = HEAD_DIM // 2
    inverse = ROPE_THETA ** (-(jnp.arange(half_width, dtype=jnp.float32) * 2.0) / HEAD_DIM)
    angle_half = positions.astype(jnp.float32)[:, None] * inverse[None, :]
    angle_full = jnp.concatenate([angle_half, angle_half], axis=-1)
    return (jnp.cos(angle_full), jnp.sin(angle_full))


def rotate_half(values):
    half_width = values.shape[-1] // 2
    return jnp.concatenate([-values[..., half_width:], values[..., :half_width]], axis=-1)


def rotate_back(values):
    half_width = values.shape[-1] // 2
    return jnp.concatenate([values[..., half_width:], -values[..., :half_width]], axis=-1)


def apply_rope(values, cosine, sine_table):
    return values * cosine[:, None, :] + rotate_half(values) * sine_table[:, None, :]


def undo_rope(grads, cosine, sine_table):
    return grads * cosine[:, None, :] + rotate_back(grads * sine_table[:, None, :])


def rms_forward(values, gain):
    inv_scale = lax.rsqrt(jnp.mean(values * values, axis=-1, keepdims=True) + EPSILON)
    normed = values * inv_scale
    return (normed, inv_scale, normed * gain)


def rms_backward(grads, normed, inv_scale, gain):
    through = grads * gain
    inner = jnp.mean(through * normed, axis=-1, keepdims=True)
    return (inv_scale * (through - normed * inner), jnp.sum(grads * normed, axis=0))


def spans(first, count, size):
    cuts = []
    at = first
    while at < first + count:
        end = min((at // size + 1) * size, first + count)
        cuts.append((at // size, at % size, at - first, end - at))
        at = end
    return cuts


def kept_of(index, ff_block, ff_own):
    at = min(index * ff_block, ff_own - ff_block)
    return (at, min(index * ff_block - at, ff_block))


def weight_sums(mlp_rows, cot_rows, hidden_low, grad_gate, grad_up, zs, shards):
    tokens, width = mlp_rows.shape
    units = hidden_low.shape[1]
    rows = width // zs
    d_z = width // shards // zs
    f_z = units // zs

    def kernel(x_ref, cot_ref, hidden_ref, gate_ref, up_ref, out_ref):
        def chunks(size):
            return [(at, min(256, size - at)) for at in range(0, size, 256)]

        def column_sum(left, right_ref):
            got = jnp.dot(left, right_ref[...], preferred_element_type=jnp.float32)
            return got.astype(jnp.bfloat16)

        for first, wide in chunks(units):
            got = column_sum(hidden_ref[:, first : first + wide].T, cot_ref)
            for z, row, at, count in spans(first, wide, f_z):
                for tile in range(width // 128):
                    piece = got[at : at + count, tile * 128 : (tile + 1) * 128]
                    for to, to_row, from_row, length in spans(tile * f_z + row, count, rows):
                        out_ref[z, 0, to_row : to_row + length, to * 128 : (to + 1) * 128] = piece[
                            from_row : from_row + length
                        ]
        for first, wide in chunks(width):
            left = x_ref[:, first : first + wide].T
            for index, right_ref in ((1, gate_ref), (2, up_ref)):
                got = column_sum(left, right_ref)
                for part, row, at, count in spans(first, wide, d_z):
                    to_row = part // zs * d_z + row
                    out_ref[part % zs, index, to_row : to_row + count] = got[at : at + count]

    operands = (mlp_rows, cot_rows, hidden_low, grad_gate, grad_up)
    return pl.pallas_call(
        kernel,
        out_shape=jax.ShapeDtypeStruct((zs, 3, rows, units), jnp.bfloat16),
        in_specs=[pl.BlockSpec(memory_space=pltpu.VMEM)] * 5,
        out_specs=pl.BlockSpec(memory_space=pltpu.VMEM),
        compiler_params=pltpu.CompilerParams(vmem_limit_bytes=48 * 1024 * 1024),
        cost_estimate=pl.CostEstimate(
            flops=6 * tokens * width * units, bytes_accessed=12 * 1024 * 1024, transcendentals=0
        ),
        name="weight_sums",
    )(*operands)


def weights_in_place(all_all, shards, ff_own):
    zs, blocks, _, rows, units = all_all.shape
    width = rows * zs
    d_z = rows // shards
    f_z = units // zs

    def kernel(all_ref, gate_ref, up_ref, down_ref, wide_ref, sems):
        z = pl.program_id(0)
        for index in range(blocks):
            for tile in range(width // 128):
                for part, row, at, count in spans(tile * f_z, f_z, rows):
                    wide_ref[index, at : at + count, tile * 128 : (tile + 1) * 128] = all_ref[
                        0, index, 0, row : row + count, part * 128 : (part + 1) * 128
                    ].astype(jnp.float32)

        def move(index, skip):
            at = kept_of(index, units, ff_own)[0]
            to = pl.multiple_of(at + z * f_z + skip, 8)
            return pltpu.make_async_copy(
                wide_ref.at[index, pl.ds(skip, f_z - skip)],
                down_ref.at[pl.ds(to, f_z - skip)],
                sems.at[index],
            )

        def each_move(act):
            for index in range(blocks):
                dropped = kept_of(index, units, ff_own)[1]
                for place in range(zs):
                    skip = min(max(dropped - place * f_z, 0), f_z)
                    if skip < f_z:

                        @pl.when(z == place)
                        def _(index=index, skip=skip):
                            act(move(index, skip))

        each_move(lambda copy: copy.start())
        for number, out_ref in ((1, gate_ref), (2, up_ref)):
            for owner in range(shards):
                for index in range(blocks):
                    at, skip = kept_of(index, units, ff_own)
                    if skip < units:
                        out_ref[:, owner * ff_own + at + skip : owner * ff_own + at + units] = all_ref[
                            0, index, number, owner * d_z : (owner + 1) * d_z, skip:
                        ].astype(jnp.float32)
        each_move(lambda copy: copy.wait())

    wide = jax.ShapeDtypeStruct((d_z * zs, shards * ff_own), jnp.float32)
    return pl.pallas_call(
        kernel,
        grid=(zs,),
        out_shape=(wide, wide, jax.ShapeDtypeStruct((ff_own, width), jnp.float32)),
        in_specs=[pl.BlockSpec((1, blocks, 3, rows, units), lambda z: (z, 0, 0, 0, 0))],
        out_specs=(
            pl.BlockSpec((d_z, shards * ff_own), lambda z: (z, 0)),
            pl.BlockSpec((d_z, shards * ff_own), lambda z: (z, 0)),
            pl.BlockSpec(memory_space=pl.ANY),
        ),
        scratch_shapes=[
            pltpu.VMEM((blocks, f_z, width), jnp.float32),
            pltpu.SemaphoreType.DMA((blocks,)),
        ],
        compiler_params=pltpu.CompilerParams(vmem_limit_bytes=48 * 1024 * 1024),
        cost_estimate=pl.CostEstimate(flops=0, bytes_accessed=44 * 1024 * 1024, transcendentals=0),
        name="weights_in_place",
    )(all_all)


def prior_rows(rows, back_reach):
    parts = []
    for distance in range(back_reach, 0, -1):
        parts.append(passed_along(rows, ("rep", "shard"), distance))
    parts.append(rows)
    return jnp.concatenate(parts, axis=0)


def return_rows(grads, tok_rows, back_reach):
    total = grads[back_reach * tok_rows :]
    for distance in range(back_reach, 0, -1):
        first_row = (back_reach - distance) * tok_rows
        total = total + passed_along(
            grads[first_row : first_row + tok_rows], ("rep", "shard"), -distance
        )
    return total


def token_sum(left, right):
    return lax.dot_general(
        left, right, (((0,), (0,)), ((), ())), preferred_element_type=jnp.float32
    ).astype(jnp.bfloat16)


def per_device(
    hidden_in,
    segments,
    attn_gain,
    w_query,
    b_query,
    w_key,
    b_key,
    w_value,
    b_value,
    w_out,
    mlp_gain,
    w_gate,
    w_up,
    w_down,
    cotangent,
):
    tok_rows = hidden_in.shape[0]
    back_reach = (SEQ - 2) // tok_rows + 1
    head_group = HEADS // KV_HEADS
    kv_width = KV_HEADS * HEAD_DIM
    qkv_width = D + 2 * kv_width
    scale = 1.0 / math.sqrt(HEAD_DIM)
    place = own_place()
    core, shard = place["core"], place["shard"]
    shards = lax.axis_size("shard")
    zs, ys = rep_sizes()
    d_own = D // shards
    shard_steps, y_steps, z_steps, core_steps = [
        steps_of(axis) for axis in ("shard", "y", "z", "core")
    ]
    group_steps = shard_steps + y_steps + core_steps

    ff_own = w_down.shape[0]
    blocks = ys * CORES
    ff_block = min(ff_own, -(-ff_own // (blocks * 128)) * 128)
    block = place["y"] * CORES + core
    block_at = jnp.minimum(block * ff_block, ff_own - ff_block)

    w_qkv = jnp.concatenate([w_query, w_key, w_value], axis=1)
    qkv_half = jnp.concatenate(
        [
            pick(weight.reshape(CORES, d_own // CORES, -1), core)
            for weight in (w_query, w_key, w_value)
        ],
        axis=1,
    )
    small = jnp.concatenate([attn_gain, b_query, b_key, b_value, mlp_gain])
    own_segments = segments + 1
    group_is_reach = shards == 2 and CORES * shards == back_reach
    window_at = (core * shards + shard) * tok_rows

    def window(rows):
        rows = rows.reshape((2 * back_reach * tok_rows,) + rows.shape[4:])
        return lax.dynamic_slice_in_dim(rows, window_at, (back_reach + 1) * tok_rows, 0)

    def as_rows(vector, count):
        return jnp.pad(vector, (0, count * qkv_width - vector.shape[0])).reshape(count, qkv_width)

    def columns_of(weight, owner):
        return lax.dynamic_slice_in_dim(weight, owner * ff_own + block_at, ff_block, 1)

    columns_sent = [
        pick(
            columns_of(weight, (shard + 1) % shards).reshape(2, d_own // 2, ff_block),
            own_bit(place, z_steps[0]),
        )
        for weight in (w_gate, w_up)
    ]
    if group_is_reach:
        got_qkv = swap(qkv_half, shard_steps[0])
        far = passed_along(own_segments, ("rep", "shard"), back_reach)
        both = jnp.concatenate([far, own_segments]).astype(jnp.bfloat16)
        got_small = swap(jnp.concatenate([small, both]), shard_steps[0])
        small_all = ordered(small[None], got_small[None, : small.shape[0]], place, shard_steps[0])
        got_both = got_small[small.shape[0] :].reshape(2, 1, tok_rows)
        both = ordered(both.reshape(2, 1, tok_rows), got_both, place, shard_steps[0], 1)
        got_qkv = after(got_qkv, both, *columns_sent)
        sent = as_rows(both.reshape(-1), 16)
        other_qkv = swap(jnp.concatenate([got_qkv, sent], axis=0), core_steps[0])
        got_both = other_qkv[-16:].reshape(-1)[: both.size].reshape(2, 1, shards, tok_rows)
        both = ordered(both[:, None], got_both, place, core_steps[0], 1)
        ext_segments = window(both.reshape(both.shape)).astype(jnp.int32)
        other_qkv = ordered(got_qkv, other_qkv[:-16], place, core_steps[0])
        full_qkv = ordered(w_qkv, other_qkv, place, shard_steps[0])
    else:
        small_all = gather(small[None], place, shard_steps)
        ext_segments = prior_rows(own_segments, back_reach)
        got_qkv = w_qkv
        full_qkv = lax.all_gather(w_qkv, "shard", axis=0, tiled=True)
    kv_own = kv_width // shards
    cuts = [0, d_own, 2 * d_own, 2 * d_own + kv_own, 2 * d_own + 2 * kv_own, small.shape[0]]
    gain_low, bias_query, bias_key, bias_value, mlp_low = [
        small_all[:, a:b].reshape(-1) for a, b in zip(cuts[:-1], cuts[1:])
    ]
    bias_qkv = jnp.concatenate([bias_query, bias_key, bias_value]).astype(jnp.float32)

    ext_len = ext_segments.shape[0]
    column = jnp.arange(ext_len, dtype=jnp.int32)
    row_at = back_reach * tok_rows + jnp.arange(tok_rows, dtype=jnp.int32)
    same_doc = own_segments[:, None] == ext_segments[None, :]
    doc_first = jnp.min(jnp.where(same_doc, column[None, :], ext_len), axis=1)
    positions = row_at - doc_first
    allowed = same_doc & (column[None, :] <= row_at[:, None])
    cosine, sine_table = rope_tables(positions)
    input_wide = hidden_in.astype(jnp.float32)
    gain_attn = gain_low.astype(jnp.float32)
    gain_mlp = mlp_low.astype(jnp.float32)
    normed_attn, inv_attn, scaled_attn = rms_forward(input_wide, gain_attn)
    attn_input = scaled_attn.astype(jnp.bfloat16)

    def all_rows(own, fetched):
        if shards == 2:
            for step in y_steps:
                fetched = ordered(fetched, swap(fetched, step), place, step)
            other = ordered(fetched, swap(fetched, core_steps[0]), place, core_steps[0])
            return ordered(own, other, place, shard_steps[0])
        return lax.all_gather(own, "shard", axis=0, tiled=True)


    def all_block_rows(weight, got):
        if shards == 2:
            other = ordered(got, swap(got, z_steps[0]), place, z_steps[0])
            return (ordered(columns_of(weight, shard), other, place, shard_steps[0]), other)
        sent = jnp.stack([columns_of(weight, owner) for owner in range(shards)])
        got = lax.all_to_all(sent, "shard", split_axis=0, concat_axis=0, tiled=True)
        return (got.reshape(D, ff_block), got)

    out_part = pick(w_out.reshape(CORES, ys, d_own // CORES // ys, D), core)
    out_part = pick(out_part, place["y"])
    got_out = swap(after(out_part, got_qkv), shard_steps[0])
    cot_shards = group_tokens(after(cotangent, got_qkv), shard_steps)
    got_gate, got_up = [swap(after(sent, got_qkv), shard_steps[0]) for sent in columns_sent]
    down_rows = lax.dynamic_slice_in_dim(w_down, block_at, ff_block, 0)
    once = block_at + jnp.arange(ff_block, dtype=jnp.int32) >= block * ff_block
    down_here = jnp.where(once[:, None], down_rows, jnp.zeros_like(down_rows))

    qkv_lin = jnp.dot(attn_input, full_qkv, preferred_element_type=jnp.float32) + bias_qkv
    rot = apply_rope(
        qkv_lin[:, : D + kv_width].reshape(tok_rows, HEADS + KV_HEADS, HEAD_DIM), cosine, sine_table
    ).astype(jnp.bfloat16)
    query_rot = rot[:, :HEADS]
    value_low = qkv_lin[:, D + kv_width :].astype(jnp.bfloat16)
    kv_own_rows = jnp.concatenate([rot[:, HEADS:].reshape(tok_rows, kv_width), value_low], axis=1)
    if group_is_reach:
        far = passed_along(kv_own_rows, ("rep", "shard"), back_reach)
        both = jnp.stack([far, kv_own_rows])[:, None]
        kv_sent = both
        both = ordered(both, swap(both, shard_steps[0]), place, shard_steps[0], 1)[:, None]
        both = ordered(both, swap(both, core_steps[0]), place, core_steps[0], 1)
        kv_ext = window(both)
    else:
        kv_ext = prior_rows(kv_own_rows, back_reach)
        kv_sent = kv_ext
    full_out = all_rows(w_out, after(got_out, kv_sent))
    gate_here, other_gate = all_block_rows(w_gate, after(got_gate, kv_sent))
    up_here, other_up = all_block_rows(w_up, after(got_up, kv_sent))
    cot_ys = group_tokens(after(cot_shards, kv_sent), y_steps)
    cot_rows = group_tokens(cot_ys, core_steps)
    keys_ext = kv_ext[:, :kv_width].reshape(ext_len, KV_HEADS, HEAD_DIM)
    values_ext = kv_ext[:, kv_width:].reshape(ext_len, KV_HEADS, HEAD_DIM)
    queries = query_rot.reshape(tok_rows, KV_HEADS, head_group, HEAD_DIM)
    scores = (
        jnp.einsum("qkgd,wkd->kgqw", queries, keys_ext, preferred_element_type=jnp.float32) * scale
    )
    scores = jnp.where(allowed[None, None], scores, MASKED)
    row_max = jnp.max(scores, axis=-1, keepdims=True)
    raw_weights = jnp.exp(scores - row_max)
    row_total = jnp.sum(raw_weights, axis=-1, keepdims=True)
    probs_low = (raw_weights / row_total).astype(jnp.bfloat16)
    log_total = row_max + jnp.log(row_total)
    attn_rows = jnp.einsum(
        "kgqw,wkd->qkgd", probs_low, values_ext, preferred_element_type=jnp.float32
    ).astype(jnp.bfloat16)
    attn_out = after(attn_rows.reshape(tok_rows, D), got_gate, got_up, cot_shards)
    attn_rows = attn_out.reshape(attn_rows.shape)
    after_attn = input_wide + jnp.dot(attn_out, full_out, preferred_element_type=jnp.float32)
    normed_mlp, inv_mlp, scaled_mlp = rms_forward(after_attn, gain_mlp)
    mlp_input = scaled_mlp.astype(jnp.bfloat16)

    mlp_rows = group_tokens(mlp_input, shard_steps)
    mlp_rows = group_tokens(after(mlp_rows, other_gate, other_up, cot_ys), y_steps)
    mlp_rows = group_tokens(after(mlp_rows, cot_rows), core_steps)
    gate_lin = jnp.dot(mlp_rows, gate_here, preferred_element_type=jnp.float32)
    up_lin = jnp.dot(mlp_rows, up_here, preferred_element_type=jnp.float32)
    gate_sig = jax.nn.sigmoid(gate_lin)
    gate_act = gate_lin * gate_sig
    hidden_low = (gate_act * up_lin).astype(jnp.bfloat16)
    z_halves = (2,) * len(z_steps)
    grad_hidden = jnp.einsum("td,fd->tf", cot_rows, down_here, preferred_element_type=jnp.float32)
    grad_gate_lin = (grad_hidden * up_lin * gate_sig * (1.0 + gate_lin * (1.0 - gate_sig))).astype(
        jnp.bfloat16
    )
    grad_up_lin = (grad_hidden * gate_act).astype(jnp.bfloat16)
    by_tiles = (d_own // zs) % 16 == 0 and (ff_block // zs) % 16 == 0 and ff_own % 128 == 0
    if by_tiles:
        all_parts = weight_sums(
            mlp_rows, cot_rows, hidden_low, grad_gate_lin, grad_up_lin, zs, shards
        )
    else:
        down_parts = token_sum(hidden_low, cot_rows)
        gate_parts = token_sum(mlp_rows, grad_gate_lin)
        up_parts = token_sum(mlp_rows, grad_up_lin)
    normed_parts = jnp.einsum(
        "tf,df->td", grad_gate_lin, gate_here, preferred_element_type=jnp.float32
    ) + jnp.einsum(
        "tf,df->td",
        grad_up_lin,
        up_here,
        preferred_element_type=jnp.float32,
    )
    block_rows_out = D // zs
    tiles_in, tiles_out = D // 128, ff_block // 128

    def as_block(parts):
        parts = parts.reshape(zs, ff_block // zs, tiles_in, 128).transpose(0, 2, 1, 3)
        parts = parts.reshape(zs, tiles_out, block_rows_out, 128).transpose(0, 2, 1, 3)
        return parts.reshape(zs, block_rows_out, ff_block)

    def from_block(whole):
        lead = whole.shape[:-2]
        whole = whole.reshape(lead + (block_rows_out, tiles_out, 128)).swapaxes(-3, -2)
        whole = whole.reshape(lead + (tiles_in, ff_block // zs, 128)).swapaxes(-3, -2)
        return whole.reshape(lead + (ff_block // zs, D))

    def by_z(parts):
        parts = parts.reshape(shards, zs, d_own // zs, ff_block).swapaxes(0, 1)
        return parts.reshape(zs, block_rows_out, ff_block)

    if not by_tiles:
        all_parts = jnp.stack([as_block(down_parts), by_z(gate_parts), by_z(up_parts)], axis=1)
    same_yc = [[z * blocks + index for z in range(zs)] for index in range(blocks)]
    all_sum = lax.psum_scatter(
        all_parts, "rep", scatter_dimension=0, axis_index_groups=same_yc, tiled=False
    )
    grad_mlp_normed = group_sum(normed_parts, group_steps)

    def from_rep(piece):
        whole = lax.all_gather(piece, "rep", axis=0)
        return whole.reshape((zs, blocks) + piece.shape)

    grad_part, grad_mlp_gain = rms_backward(grad_mlp_normed, normed_mlp, inv_mlp, gain_mlp)
    grad_after = cotangent.astype(jnp.float32) + grad_part
    after_low = grad_after.astype(jnp.bfloat16)
    out_parts = jnp.dot(
        after(hidden_low, after_low), down_here, preferred_element_type=jnp.float32
    )
    out_sums = group_sum(out_parts, y_steps + core_steps)

    def half_sum(left, right):
        columns = left.reshape(tok_rows, shards, CORES, d_own // CORES)
        kept, sent = pick(columns, core, 2), pick(columns, 1 - core, 2)
        columns = jnp.concatenate([kept, swap(sent, core_steps[0])], axis=0)
        right = jnp.concatenate([right, swap(right, core_steps[0])], axis=0)
        return token_sum(columns.reshape(CORES * tok_rows, -1), right)

    def shard_scatter(parts):
        parts = parts.reshape((shards, -1, parts.shape[1]))
        if shards == 2:
            return scatter(parts, place, shard_steps)
        return lax.psum_scatter(parts, "shard", scatter_dimension=0)

    out_sum = shard_scatter(half_sum(attn_out, after_low))
    grad_attn_out = jnp.einsum(
        "te,de->td", after_low, full_out, preferred_element_type=jnp.float32
    ).astype(jnp.bfloat16)
    grad_rows = grad_attn_out.reshape(tok_rows, KV_HEADS, head_group, HEAD_DIM)
    soft_probs = jnp.exp(scores - log_total)
    probs_back = soft_probs.astype(jnp.bfloat16)
    grad_values_ext = jnp.einsum(
        "kgqw,qkgd->wkd", probs_back, grad_rows, preferred_element_type=jnp.float32
    )
    grad_probs = jnp.einsum(
        "qkgd,wkd->kgqw", grad_rows, values_ext, preferred_element_type=jnp.float32
    )
    delta = jnp.sum(grad_rows.astype(jnp.float32) * attn_rows.astype(jnp.float32), axis=-1)
    delta = jnp.transpose(delta, (1, 2, 0))[..., None]
    grad_scores = (soft_probs * (grad_probs - delta) * scale).astype(jnp.bfloat16)
    grad_queries = jnp.einsum(
        "kgqw,wkd->qkgd", grad_scores, keys_ext, preferred_element_type=jnp.float32
    )
    grad_keys_ext = jnp.einsum(
        "kgqw,qkgd->wkd", grad_scores, queries, preferred_element_type=jnp.float32
    )
    grads_ext = jnp.concatenate(
        [grad_keys_ext.reshape(ext_len, kv_width), grad_values_ext.reshape(ext_len, kv_width)],
        axis=1,
    )
    grads_ext = after(grads_ext, out_sum, out_sums)
    layer_out = after_attn + group_sum(out_sums, shard_steps)
    grad_kv = return_rows(grads_ext, tok_rows, back_reach)
    in_sum = all_sum[1:].reshape(2, shards, d_own // zs, ff_block).swapaxes(0, 1)
    in_piece = exchange(in_sum, place, grads_ext).swapaxes(0, 1)
    all_piece = jnp.concatenate(
        [all_sum[:1], in_piece.reshape(2, block_rows_out, ff_block)], axis=0
    )
    all_all = from_rep(all_piece)
    grad_query_lin = undo_rope(
        grad_queries.reshape(tok_rows, HEADS, HEAD_DIM), cosine, sine_table
    ).reshape(tok_rows, D)
    grad_key_lin = undo_rope(
        grad_kv[:, :kv_width].reshape(tok_rows, KV_HEADS, HEAD_DIM), cosine, sine_table
    ).reshape(tok_rows, kv_width)
    grad_qkv = jnp.concatenate([grad_query_lin, grad_key_lin, grad_kv[:, kv_width:]], axis=1)
    grad_b_qkv = jnp.sum(grad_qkv, axis=0)
    qkv_low = after(grad_qkv.astype(jnp.bfloat16), layer_out)
    grad_attn_normed = jnp.einsum(
        "te,de->td", qkv_low, full_qkv, preferred_element_type=jnp.float32
    )
    grad_front, grad_attn_gain = rms_backward(grad_attn_normed, normed_attn, inv_attn, gain_attn)
    grad_input = grad_after + grad_front

    vectors = jnp.concatenate([grad_attn_gain, grad_b_qkv, grad_mlp_gain])
    vectors = vectors + swap(vectors, core_steps[0])
    ends = [0, D, 2 * D, 2 * D + kv_width, qkv_width + D, qkv_width + 2 * D]
    vectors = jnp.concatenate(
        [vectors[a:b].reshape(shards, -1) for a, b in zip(ends[:-1], ends[1:])], axis=1
    )
    vectors = pick(vectors.reshape(shards, CORES, zs, 1, -1), core, 1).astype(jnp.bfloat16)
    vector_len = vectors.shape[-1]
    piece_rows = d_own // CORES // zs
    below = 16 - piece_rows % 16
    vectors = jnp.pad(vectors, ((0, 0), (0, 0), (0, below - 1), (0, qkv_width - vector_len)))
    query_parts = half_sum(attn_input, qkv_low).reshape(shards, zs, piece_rows, qkv_width)
    query_parts = jnp.concatenate([query_parts, vectors], axis=2)
    query_sum = shard_scatter(query_parts.reshape(-1, qkv_width))
    out_sum = out_sum.reshape(zs, piece_rows, D)
    out_sum = jnp.pad(out_sum, ((0, 0), (0, below), (0, 0))).reshape(-1, D)
    parts = jnp.concatenate([query_sum.reshape(-1, qkv_width), out_sum], axis=1)
    y_halves = (2,) * len(y_steps)
    parts = scatter(parts.reshape(parts.shape[:1] + y_halves + (-1,)), place, y_steps, 1)
    piece = scatter(parts.reshape(z_halves + (-1, parts.shape[1])), place, z_steps)
    for index, step in enumerate(y_steps[::-1]):
        mine = jnp.expand_dims(piece, index + 1)
        got = jnp.expand_dims(swap(piece, step), index + 1)
        piece = ordered(mine, got, place, step, index + 1)
    piece = piece.reshape(piece.shape[0], -1)
    if by_tiles:
        final_gate, final_up, final_down = weights_in_place(all_all, shards, ff_own)
    attn_half = piece
    for index, step in enumerate(z_steps[::-1]):
        mine = jnp.expand_dims(attn_half, index)
        got = jnp.expand_dims(swap(attn_half, step), index)
        if by_tiles and index == len(z_steps) - 1:
            got = after(got, final_down)
        attn_half = ordered(mine, got, place, step, index)
    attn_half = attn_half.reshape(-1, attn_half.shape[-1])
    attn_other = swap(attn_half, core_steps[0])
    attn_all = ordered(attn_half, attn_other, place, core_steps[0])
    attn_all = attn_all.reshape(CORES * zs, piece_rows + below, qkv_width + D)
    vector_own = attn_all[:, piece_rows, :vector_len].reshape(-1).astype(jnp.float32)
    attn_all = attn_all[:, :piece_rows].reshape(d_own, qkv_width + D)
    edges = [0, D, D + kv_width, qkv_width, qkv_width + D]
    final_query, final_key, final_value, final_out = [
        attn_all[:, a:b].astype(jnp.float32) for a, b in zip(edges[:-1], edges[1:])
    ]
    final_gain, final_bq, final_bk, final_bv, final_mlp_gain = [
        vector_own[a:b] for a, b in zip(cuts[:-1], cuts[1:])
    ]

    if not by_tiles:
        kept = [slice(kept_of(index, ff_block, ff_own)[1], ff_block) for index in range(blocks)]
        down_all = from_block(all_all[:, :, 0])
        in_all = all_all[:, :, 1:].reshape(zs, blocks, 2, shards, d_own // zs, ff_block)

        def in_place(pieces):
            columns = []
            for owner in range(shards):
                for index in range(blocks):
                    whole = pieces[:, index, owner].reshape(d_own, ff_block)
                    columns.append(whole[:, kept[index]])
            return jnp.concatenate(columns, axis=1).astype(jnp.float32)

        final_down = jnp.concatenate(
            [down_all[:, index].reshape(ff_block, D)[kept[index]] for index in range(blocks)], axis=0
        ).astype(jnp.float32)
        final_gate = in_place(in_all[:, :, 0])
        final_up = in_place(in_all[:, :, 1])
    return (
        layer_out,
        grad_input,
        final_gain,
        final_query,
        final_bq,
        final_key,
        final_bk,
        final_value,
        final_bv,
        final_out,
        final_mlp_gain,
        final_gate,
        final_up,
        final_down,
    )


def solution(mesh):
    return jax.shard_map(
        per_device,
        mesh=mesh,
        in_specs=(
            P(("rep", "shard"), None),
            P(("rep", "shard")),
            P("shard"),
            P("shard", None),
            P("shard"),
            P("shard", None),
            P("shard"),
            P("shard", None),
            P("shard"),
            P("shard", None),
            P("shard"),
            P("shard", None),
            P("shard", None),
            P("shard", None),
            P(("rep", "shard"), None),
        ),
        out_specs=(
            P(("rep", "shard"), None),
            P(("rep", "shard"), None),
            P("shard"),
            P("shard", None),
            P("shard"),
            P("shard", None),
            P("shard"),
            P("shard", None),
            P("shard"),
            P("shard", None),
            P("shard"),
            P("shard", None),
            P("shard", None),
            P("shard", None),
        ),
        check_vma=False,
    )
```

```python
import math

import jax
import jax.numpy as jnp
from jax import lax
from jax.experimental import pallas as pl
from jax.experimental.pallas import tpu as pltpu
from jax.sharding import PartitionSpec as P

D = 896
HEADS = 14
KV_HEADS = 2
HEAD_DIM = 64
SEQ = 512


EPSILON = 1e-06
ROPE_THETA = 1000000.0
MASKED = -1e30

CORES = 2
ALONG_Z = 4


def passed_along(shard, axis, by):
    peers = lax.axis_size(axis)
    pairs = [(i, i + by) for i in range(peers) if 0 <= i + by < peers]
    return lax.ppermute(shard, axis, pairs)


def rep_sizes():
    planes = lax.axis_size("rep") // CORES
    zs = min(ALONG_Z, planes)
    return (zs, planes // zs)


def own_place():
    zs, ys = rep_sizes()
    rep = lax.axis_index("rep")
    plane = rep // CORES
    return {"z": plane // ys, "y": plane % ys, "core": rep % CORES, "shard": lax.axis_index("shard")}


def steps_of(axis):
    zs, ys = rep_sizes()
    size = {"z": zs, "y": ys, "core": CORES, "shard": lax.axis_size("shard")}[axis]
    return [(axis, 1 << i) for i in range(size.bit_length() - 1)]


def swap(value, step):
    axis, bit = step
    if axis == "shard":
        peers = lax.axis_size("shard")
        return lax.ppermute(value, "shard", [(i, i ^ bit) for i in range(peers)])
    zs, ys = rep_sizes()
    pairs = []
    for rep in range(zs * ys * CORES):
        at = {"z": rep // CORES // ys, "y": rep // CORES % ys, "core": rep % CORES}
        at[axis] ^= bit
        pairs.append((rep, (at["z"] * ys + at["y"]) * CORES + at["core"]))
    return lax.ppermute(value, "rep", pairs)


def own_bit(place, step):
    return place[step[0]] // step[1] % 2


def nothing(*refs):
    pass


def after(value, *earlier):
    anywhere = pl.BlockSpec(memory_space=pl.ANY)
    return pl.pallas_call(
        nothing,
        out_shape=jax.ShapeDtypeStruct(value.shape, value.dtype),
        in_specs=[anywhere] * (1 + len(earlier)),
        out_specs=anywhere,
        input_output_aliases={0: 0},
        cost_estimate=pl.CostEstimate(flops=0, bytes_accessed=0, transcendentals=0),
        name="after",
    )(value, *earlier)


def pick(whole, at, axis=0):
    return lax.dynamic_index_in_dim(whole, at, axis, keepdims=False)


def ordered(mine, got, place, step, axis=0):
    first = own_bit(place, step) == 0
    return jnp.where(
        first, jnp.concatenate([mine, got], axis=axis), jnp.concatenate([got, mine], axis=axis)
    )


def gather(piece, place, steps):
    for step in steps:
        piece = ordered(piece, swap(piece, step), place, step)
    return piece


def scatter_step(parts, place, step, axis=0, earlier=()):
    at = own_bit(place, step)
    got = swap(pick(parts, 1 - at, axis), step)
    if earlier:
        got = after(got, *earlier)
    total = pick(parts, at, axis).astype(jnp.float32) + got.astype(jnp.float32)
    return total.astype(jnp.bfloat16)


def scatter(parts, place, steps, lead=0, earlier=()):
    for index, step in enumerate(steps):
        parts = scatter_step(
            parts, place, step, lead + len(steps) - 1 - index, earlier[index : index + 1]
        )
    return parts


def exchange(parts, place, earlier):
    shards = lax.axis_size("shard")
    if shards == 2:
        at = place["shard"]
        got = after(swap(pick(parts, 1 - at), ("shard", 1)), earlier)
        return ordered(pick(parts, at)[None], got[None], place, ("shard", 1))
    return lax.all_to_all(parts, "shard", split_axis=0, concat_axis=0, tiled=True)


def group_tokens(rows, steps):
    for step in steps:
        rows = jnp.concatenate([rows, swap(rows, step)], axis=0)
    return rows


def group_step(parts, step, earlier=()):
    half = parts.shape[0] // 2
    sent = parts[half:]
    if step[0] != "core":
        sent = sent.astype(jnp.bfloat16)
    got = swap(sent, step)
    if earlier:
        got = after(got, *earlier)
    return parts[:half] + got.astype(jnp.float32)


def group_sum(parts, steps):
    for step in steps[::-1]:
        parts = group_step(parts, step)
    return parts


def rope_tables(positions):
    half_width = HEAD_DIM // 2
    inverse = ROPE_THETA ** (-(jnp.arange(half_width, dtype=jnp.float32) * 2.0) / HEAD_DIM)
    angle_half = positions.astype(jnp.float32)[:, None] * inverse[None, :]
    angle_full = jnp.concatenate([angle_half, angle_half], axis=-1)
    return (jnp.cos(angle_full), jnp.sin(angle_full))


def rotate_half(values):
    half_width = values.shape[-1] // 2
    return jnp.concatenate([-values[..., half_width:], values[..., :half_width]], axis=-1)


def rotate_back(values):
    half_width = values.shape[-1] // 2
    return jnp.concatenate([values[..., half_width:], -values[..., :half_width]], axis=-1)


def apply_rope(values, cosine, sine_table):
    return values * cosine[:, None, :] + rotate_half(values) * sine_table[:, None, :]


def undo_rope(grads, cosine, sine_table):
    return grads * cosine[:, None, :] + rotate_back(grads * sine_table[:, None, :])


def rms_forward(values, gain):
    inv_scale = lax.rsqrt(jnp.mean(values * values, axis=-1, keepdims=True) + EPSILON)
    normed = values * inv_scale
    return (normed, inv_scale, normed * gain)


def rms_backward(grads, normed, inv_scale, gain):
    through = grads * gain
    inner = jnp.mean(through * normed, axis=-1, keepdims=True)
    return (inv_scale * (through - normed * inner), jnp.sum(grads * normed, axis=0))


def spans(first, count, size):
    cuts = []
    at = first
    while at < first + count:
        end = min((at // size + 1) * size, first + count)
        cuts.append((at // size, at % size, at - first, end - at))
        at = end
    return cuts


def kept_of(index, ff_block, ff_own):
    at = min(index * ff_block, ff_own - ff_block)
    return (at, min(index * ff_block - at, ff_block))


def weight_sums(mlp_rows, cot_rows, hidden_low, grad_gate, grad_up, zs, shards):
    tokens, width = mlp_rows.shape
    units = hidden_low.shape[1]
    rows = width // zs
    d_z = width // shards // zs
    f_z = units // zs

    def kernel(x_ref, cot_ref, hidden_ref, gate_ref, up_ref, out_ref):
        def chunks(size):
            return [(at, min(256, size - at)) for at in range(0, size, 256)]

        def column_sum(left, right_ref):
            got = jnp.dot(left, right_ref[...], preferred_element_type=jnp.float32)
            return got.astype(jnp.bfloat16)

        for first, wide in chunks(units):
            got = column_sum(hidden_ref[:, first : first + wide].T, cot_ref)
            for z, row, at, count in spans(first, wide, f_z):
                for tile in range(width // 128):
                    piece = got[at : at + count, tile * 128 : (tile + 1) * 128]
                    for to, to_row, from_row, length in spans(tile * f_z + row, count, rows):
                        out_ref[z, 0, to_row : to_row + length, to * 128 : (to + 1) * 128] = piece[
                            from_row : from_row + length
                        ]
        for first, wide in chunks(width):
            left = x_ref[:, first : first + wide].T
            for index, right_ref in ((1, gate_ref), (2, up_ref)):
                got = column_sum(left, right_ref)
                for part, row, at, count in spans(first, wide, d_z):
                    to_row = part // zs * d_z + row
                    out_ref[part % zs, index, to_row : to_row + count] = got[at : at + count]

    operands = (mlp_rows, cot_rows, hidden_low, grad_gate, grad_up)
    return pl.pallas_call(
        kernel,
        out_shape=jax.ShapeDtypeStruct((zs, 3, rows, units), jnp.bfloat16),
        in_specs=[pl.BlockSpec(memory_space=pltpu.VMEM)] * 5,
        out_specs=pl.BlockSpec(memory_space=pltpu.VMEM),
        compiler_params=pltpu.CompilerParams(vmem_limit_bytes=48 * 1024 * 1024),
        cost_estimate=pl.CostEstimate(
            flops=6 * tokens * width * units, bytes_accessed=12 * 1024 * 1024, transcendentals=0
        ),
        name="weight_sums",
    )(*operands)


def weights_in_place(all_all, shards, ff_own):
    zs, blocks, _, rows, units = all_all.shape
    width = rows * zs
    d_z = rows // shards
    f_z = units // zs

    def kernel(all_ref, gate_ref, up_ref, down_ref, wide_ref, sems):
        z = pl.program_id(0)
        for index in range(blocks):
            for tile in range(width // 128):
                for part, row, at, count in spans(tile * f_z, f_z, rows):
                    wide_ref[index, at : at + count, tile * 128 : (tile + 1) * 128] = all_ref[
                        0, index, 0, row : row + count, part * 128 : (part + 1) * 128
                    ].astype(jnp.float32)

        def move(index, skip):
            at = kept_of(index, units, ff_own)[0]
            to = pl.multiple_of(at + z * f_z + skip, 8)
            return pltpu.make_async_copy(
                wide_ref.at[index, pl.ds(skip, f_z - skip)],
                down_ref.at[pl.ds(to, f_z - skip)],
                sems.at[index],
            )

        def each_move(act):
            for index in range(blocks):
                dropped = kept_of(index, units, ff_own)[1]
                for place in range(zs):
                    skip = min(max(dropped - place * f_z, 0), f_z)
                    if skip < f_z:

                        @pl.when(z == place)
                        def _(index=index, skip=skip):
                            act(move(index, skip))

        each_move(lambda copy: copy.start())
        for number, out_ref in ((1, gate_ref), (2, up_ref)):
            for owner in range(shards):
                for index in range(blocks):
                    at, skip = kept_of(index, units, ff_own)
                    if skip < units:
                        out_ref[:, owner * ff_own + at + skip : owner * ff_own + at + units] = all_ref[
                            0, index, number, owner * d_z : (owner + 1) * d_z, skip:
                        ].astype(jnp.float32)
        each_move(lambda copy: copy.wait())

    wide = jax.ShapeDtypeStruct((d_z * zs, shards * ff_own), jnp.float32)
    return pl.pallas_call(
        kernel,
        grid=(zs,),
        out_shape=(wide, wide, jax.ShapeDtypeStruct((ff_own, width), jnp.float32)),
        in_specs=[pl.BlockSpec((1, blocks, 3, rows, units), lambda z: (z, 0, 0, 0, 0))],
        out_specs=(
            pl.BlockSpec((d_z, shards * ff_own), lambda z: (z, 0)),
            pl.BlockSpec((d_z, shards * ff_own), lambda z: (z, 0)),
            pl.BlockSpec(memory_space=pl.ANY),
        ),
        scratch_shapes=[
            pltpu.VMEM((blocks, f_z, width), jnp.float32),
            pltpu.SemaphoreType.DMA((blocks,)),
        ],
        compiler_params=pltpu.CompilerParams(vmem_limit_bytes=48 * 1024 * 1024),
        cost_estimate=pl.CostEstimate(flops=0, bytes_accessed=44 * 1024 * 1024, transcendentals=0),
        name="weights_in_place",
    )(all_all)


def prior_rows(rows, back_reach):
    parts = []
    for distance in range(back_reach, 0, -1):
        parts.append(passed_along(rows, ("rep", "shard"), distance))
    parts.append(rows)
    return jnp.concatenate(parts, axis=0)


def return_rows(grads, tok_rows, back_reach):
    total = grads[back_reach * tok_rows :]
    for distance in range(back_reach, 0, -1):
        first_row = (back_reach - distance) * tok_rows
        total = total + passed_along(
            grads[first_row : first_row + tok_rows], ("rep", "shard"), -distance
        )
    return total


def token_sum(left, right):
    return lax.dot_general(
        left, right, (((0,), (0,)), ((), ())), preferred_element_type=jnp.float32
    ).astype(jnp.bfloat16)


def per_device(
    hidden_in,
    segments,
    attn_gain,
    w_query,
    b_query,
    w_key,
    b_key,
    w_value,
    b_value,
    w_out,
    mlp_gain,
    w_gate,
    w_up,
    w_down,
    cotangent,
):
    tok_rows = hidden_in.shape[0]
    back_reach = (SEQ - 2) // tok_rows + 1
    head_group = HEADS // KV_HEADS
    kv_width = KV_HEADS * HEAD_DIM
    qkv_width = D + 2 * kv_width
    scale = 1.0 / math.sqrt(HEAD_DIM)
    place = own_place()
    core, shard = place["core"], place["shard"]
    shards = lax.axis_size("shard")
    zs, ys = rep_sizes()
    d_own = D // shards
    shard_steps, y_steps, z_steps, core_steps = [
        steps_of(axis) for axis in ("shard", "y", "z", "core")
    ]
    group_steps = shard_steps + y_steps + core_steps

    ff_own = w_down.shape[0]
    blocks = ys * CORES
    ff_block = min(ff_own, -(-ff_own // (blocks * 128)) * 128)
    block = place["y"] * CORES + core
    block_at = jnp.minimum(block * ff_block, ff_own - ff_block)

    w_qkv = jnp.concatenate([w_query, w_key, w_value], axis=1)
    qkv_half = jnp.concatenate(
        [
            pick(weight.reshape(CORES, d_own // CORES, -1), core)
            for weight in (w_query, w_key, w_value)
        ],
        axis=1,
    )
    small = jnp.concatenate([attn_gain, b_query, b_key, b_value, mlp_gain])
    own_segments = segments + 1
    group_is_reach = shards == 2 and CORES * shards == back_reach
    window_at = (core * shards + shard) * tok_rows

    def window(rows):
        rows = rows.reshape((2 * back_reach * tok_rows,) + rows.shape[4:])
        return lax.dynamic_slice_in_dim(rows, window_at, (back_reach + 1) * tok_rows, 0)

    def as_rows(vector, count):
        return jnp.pad(vector, (0, count * qkv_width - vector.shape[0])).reshape(count, qkv_width)

    def columns_of(weight, owner):
        return lax.dynamic_slice_in_dim(weight, owner * ff_own + block_at, ff_block, 1)

    columns_sent = [
        pick(
            columns_of(weight, (shard + 1) % shards).reshape(2, d_own // 2, ff_block),
            own_bit(place, z_steps[0]),
        )
        for weight in (w_gate, w_up)
    ]
    if group_is_reach:
        got_qkv = swap(qkv_half, shard_steps[0])
        far = passed_along(own_segments, ("rep", "shard"), back_reach)
        both = jnp.concatenate([far, own_segments]).astype(jnp.bfloat16)
        got_small = swap(jnp.concatenate([small, both]), shard_steps[0])
        small_all = ordered(small[None], got_small[None, : small.shape[0]], place, shard_steps[0])
        got_both = got_small[small.shape[0] :].reshape(2, 1, tok_rows)
        both = ordered(both.reshape(2, 1, tok_rows), got_both, place, shard_steps[0], 1)
        got_qkv = after(got_qkv, both, *columns_sent)
        sent = as_rows(both.reshape(-1), 16)
        other_qkv = swap(jnp.concatenate([got_qkv, sent], axis=0), core_steps[0])
        got_both = other_qkv[-16:].reshape(-1)[: both.size].reshape(2, 1, shards, tok_rows)
        both = ordered(both[:, None], got_both, place, core_steps[0], 1)
        ext_segments = window(both.reshape(both.shape)).astype(jnp.int32)
        other_qkv = ordered(got_qkv, other_qkv[:-16], place, core_steps[0])
        full_qkv = ordered(w_qkv, other_qkv, place, shard_steps[0])
    else:
        small_all = gather(small[None], place, shard_steps)
        ext_segments = prior_rows(own_segments, back_reach)
        got_qkv = w_qkv
        full_qkv = lax.all_gather(w_qkv, "shard", axis=0, tiled=True)
    kv_own = kv_width // shards
    cuts = [0, d_own, 2 * d_own, 2 * d_own + kv_own, 2 * d_own + 2 * kv_own, small.shape[0]]
    gain_low, bias_query, bias_key, bias_value, mlp_low = [
        small_all[:, a:b].reshape(-1) for a, b in zip(cuts[:-1], cuts[1:])
    ]
    bias_qkv = jnp.concatenate([bias_query, bias_key, bias_value]).astype(jnp.float32)

    ext_len = ext_segments.shape[0]
    column = jnp.arange(ext_len, dtype=jnp.int32)
    row_at = back_reach * tok_rows + jnp.arange(tok_rows, dtype=jnp.int32)
    same_doc = own_segments[:, None] == ext_segments[None, :]
    doc_first = jnp.min(jnp.where(same_doc, column[None, :], ext_len), axis=1)
    positions = row_at - doc_first
    allowed = same_doc & (column[None, :] <= row_at[:, None])
    cosine, sine_table = rope_tables(positions)
    input_wide = hidden_in.astype(jnp.float32)
    gain_attn = gain_low.astype(jnp.float32)
    gain_mlp = mlp_low.astype(jnp.float32)
    normed_attn, inv_attn, scaled_attn = rms_forward(input_wide, gain_attn)
    attn_input = scaled_attn.astype(jnp.bfloat16)

    def all_rows(own, fetched):
        if shards == 2:
            for step in y_steps:
                fetched = ordered(fetched, swap(fetched, step), place, step)
            other = ordered(fetched, swap(fetched, core_steps[0]), place, core_steps[0])
            return ordered(own, other, place, shard_steps[0])
        return lax.all_gather(own, "shard", axis=0, tiled=True)


    def all_block_rows(weight, got):
        if shards == 2:
            other = ordered(got, swap(got, z_steps[0]), place, z_steps[0])
            return (ordered(columns_of(weight, shard), other, place, shard_steps[0]), other)
        sent = jnp.stack([columns_of(weight, owner) for owner in range(shards)])
        got = lax.all_to_all(sent, "shard", split_axis=0, concat_axis=0, tiled=True)
        return (got.reshape(D, ff_block), got)

    out_part = pick(w_out.reshape(CORES, ys, d_own // CORES // ys, D), core)
    out_part = pick(out_part, place["y"])
    got_out = swap(after(out_part, got_qkv), shard_steps[0])
    cot_shards = group_tokens(after(cotangent, got_qkv), shard_steps)
    got_gate, got_up = [swap(after(sent, got_qkv), shard_steps[0]) for sent in columns_sent]
    down_rows = lax.dynamic_slice_in_dim(w_down, block_at, ff_block, 0)
    once = block_at + jnp.arange(ff_block, dtype=jnp.int32) >= block * ff_block
    down_here = jnp.where(once[:, None], down_rows, jnp.zeros_like(down_rows))

    qkv_lin = jnp.dot(attn_input, full_qkv, preferred_element_type=jnp.float32) + bias_qkv
    rot = apply_rope(
        qkv_lin[:, : D + kv_width].reshape(tok_rows, HEADS + KV_HEADS, HEAD_DIM), cosine, sine_table
    ).astype(jnp.bfloat16)
    query_rot = rot[:, :HEADS]
    value_low = qkv_lin[:, D + kv_width :].astype(jnp.bfloat16)
    kv_own_rows = jnp.concatenate([rot[:, HEADS:].reshape(tok_rows, kv_width), value_low], axis=1)
    if group_is_reach:
        far = passed_along(kv_own_rows, ("rep", "shard"), back_reach)
        both = jnp.stack([far, kv_own_rows])[:, None]
        kv_sent = both
        both = ordered(both, swap(both, shard_steps[0]), place, shard_steps[0], 1)[:, None]
        both = ordered(both, swap(both, core_steps[0]), place, core_steps[0], 1)
        kv_ext = window(both)
    else:
        kv_ext = prior_rows(kv_own_rows, back_reach)
        kv_sent = kv_ext
    full_out = all_rows(w_out, after(got_out, kv_sent))
    gate_here, other_gate = all_block_rows(w_gate, after(got_gate, kv_sent))
    up_here, other_up = all_block_rows(w_up, after(got_up, kv_sent))
    cot_ys = group_tokens(after(cot_shards, kv_sent), y_steps)
    cot_rows = group_tokens(cot_ys, core_steps)
    keys_ext = kv_ext[:, :kv_width].reshape(ext_len, KV_HEADS, HEAD_DIM)
    values_ext = kv_ext[:, kv_width:].reshape(ext_len, KV_HEADS, HEAD_DIM)
    queries = query_rot.reshape(tok_rows, KV_HEADS, head_group, HEAD_DIM)
    scores = (
        jnp.einsum("qkgd,wkd->kgqw", queries, keys_ext, preferred_element_type=jnp.float32) * scale
    )
    scores = jnp.where(allowed[None, None], scores, MASKED)
    row_max = jnp.max(scores, axis=-1, keepdims=True)
    raw_weights = jnp.exp(scores - row_max)
    row_total = jnp.sum(raw_weights, axis=-1, keepdims=True)
    probs_low = (raw_weights / row_total).astype(jnp.bfloat16)
    log_total = row_max + jnp.log(row_total)
    attn_rows = jnp.einsum(
        "kgqw,wkd->qkgd", probs_low, values_ext, preferred_element_type=jnp.float32
    ).astype(jnp.bfloat16)
    attn_out = after(attn_rows.reshape(tok_rows, D), got_gate, got_up, cot_shards)
    attn_rows = attn_out.reshape(attn_rows.shape)
    after_attn = input_wide + jnp.dot(attn_out, full_out, preferred_element_type=jnp.float32)
    normed_mlp, inv_mlp, scaled_mlp = rms_forward(after_attn, gain_mlp)
    mlp_input = scaled_mlp.astype(jnp.bfloat16)

    mlp_rows = group_tokens(mlp_input, shard_steps)
    mlp_rows = group_tokens(after(mlp_rows, other_gate, other_up, cot_ys), y_steps)
    mlp_rows = group_tokens(after(mlp_rows, cot_rows), core_steps)
    gate_lin = jnp.dot(mlp_rows, gate_here, preferred_element_type=jnp.float32)
    up_lin = jnp.dot(mlp_rows, up_here, preferred_element_type=jnp.float32)
    gate_sig = jax.nn.sigmoid(gate_lin)
    gate_act = gate_lin * gate_sig
    hidden_low = (gate_act * up_lin).astype(jnp.bfloat16)
    z_halves = (2,) * len(z_steps)
    grad_hidden = jnp.einsum("td,fd->tf", cot_rows, down_here, preferred_element_type=jnp.float32)
    grad_gate_lin = (grad_hidden * up_lin * gate_sig * (1.0 + gate_lin * (1.0 - gate_sig))).astype(
        jnp.bfloat16
    )
    grad_up_lin = (grad_hidden * gate_act).astype(jnp.bfloat16)
    by_tiles = (d_own // zs) % 16 == 0 and (ff_block // zs) % 16 == 0 and ff_own % 128 == 0
    if by_tiles:
        all_parts = weight_sums(
            mlp_rows, cot_rows, hidden_low, grad_gate_lin, grad_up_lin, zs, shards
        )
    else:
        down_parts = token_sum(hidden_low, cot_rows)
        gate_parts = token_sum(mlp_rows, grad_gate_lin)
        up_parts = token_sum(mlp_rows, grad_up_lin)
    normed_parts = jnp.einsum(
        "tf,df->td", grad_gate_lin, gate_here, preferred_element_type=jnp.float32
    ) + jnp.einsum(
        "tf,df->td",
        grad_up_lin,
        up_here,
        preferred_element_type=jnp.float32,
    )
    block_rows_out = D // zs
    tiles_in, tiles_out = D // 128, ff_block // 128

    def as_block(parts):
        parts = parts.reshape(zs, ff_block // zs, tiles_in, 128).transpose(0, 2, 1, 3)
        parts = parts.reshape(zs, tiles_out, block_rows_out, 128).transpose(0, 2, 1, 3)
        return parts.reshape(zs, block_rows_out, ff_block)

    def from_block(whole):
        lead = whole.shape[:-2]
        whole = whole.reshape(lead + (block_rows_out, tiles_out, 128)).swapaxes(-3, -2)
        whole = whole.reshape(lead + (tiles_in, ff_block // zs, 128)).swapaxes(-3, -2)
        return whole.reshape(lead + (ff_block // zs, D))

    def by_z(parts):
        parts = parts.reshape(shards, zs, d_own // zs, ff_block).swapaxes(0, 1)
        return parts.reshape(zs, block_rows_out, ff_block)

    if not by_tiles:
        all_parts = jnp.stack([as_block(down_parts), by_z(gate_parts), by_z(up_parts)], axis=1)
    same_yc = [[z * blocks + index for z in range(zs)] for index in range(blocks)]
    all_sum = lax.psum_scatter(
        all_parts, "rep", scatter_dimension=0, axis_index_groups=same_yc, tiled=False
    )
    grad_mlp_normed = group_sum(normed_parts, group_steps)

    def from_rep(piece):
        whole = lax.all_gather(piece, "rep", axis=0)
        return whole.reshape((zs, blocks) + piece.shape)

    grad_part, grad_mlp_gain = rms_backward(grad_mlp_normed, normed_mlp, inv_mlp, gain_mlp)
    grad_after = cotangent.astype(jnp.float32) + grad_part
    after_low = grad_after.astype(jnp.bfloat16)
    out_parts = jnp.dot(
        after(hidden_low, after_low), down_here, preferred_element_type=jnp.float32
    )
    out_sums = group_sum(out_parts, y_steps + core_steps)

    def half_sum(left, right):
        columns = left.reshape(tok_rows, shards, CORES, d_own // CORES)
        kept, sent = pick(columns, core, 2), pick(columns, 1 - core, 2)
        columns = jnp.concatenate([kept, swap(sent, core_steps[0])], axis=0)
        right = jnp.concatenate([right, swap(right, core_steps[0])], axis=0)
        return token_sum(columns.reshape(CORES * tok_rows, -1), right)

    def shard_scatter(parts):
        parts = parts.reshape((shards, -1, parts.shape[1]))
        if shards == 2:
            return scatter(parts, place, shard_steps)
        return lax.psum_scatter(parts, "shard", scatter_dimension=0)

    out_sum = shard_scatter(half_sum(attn_out, after_low))
    grad_attn_out = jnp.einsum(
        "te,de->td", after_low, full_out, preferred_element_type=jnp.float32
    ).astype(jnp.bfloat16)
    grad_rows = grad_attn_out.reshape(tok_rows, KV_HEADS, head_group, HEAD_DIM)
    soft_probs = jnp.exp(scores - log_total)
    probs_back = soft_probs.astype(jnp.bfloat16)
    grad_values_ext = jnp.einsum(
        "kgqw,qkgd->wkd", probs_back, grad_rows, preferred_element_type=jnp.float32
    )
    grad_probs = jnp.einsum(
        "qkgd,wkd->kgqw", grad_rows, values_ext, preferred_element_type=jnp.float32
    )
    delta = jnp.sum(grad_rows.astype(jnp.float32) * attn_rows.astype(jnp.float32), axis=-1)
    delta = jnp.transpose(delta, (1, 2, 0))[..., None]
    grad_scores = (soft_probs * (grad_probs - delta) * scale).astype(jnp.bfloat16)
    grad_queries = jnp.einsum(
        "kgqw,wkd->qkgd", grad_scores, keys_ext, preferred_element_type=jnp.float32
    )
    grad_keys_ext = jnp.einsum(
        "kgqw,qkgd->wkd", grad_scores, queries, preferred_element_type=jnp.float32
    )
    grads_ext = jnp.concatenate(
        [grad_keys_ext.reshape(ext_len, kv_width), grad_values_ext.reshape(ext_len, kv_width)],
        axis=1,
    )
    layer_out = after_attn + group_sum(out_sums, shard_steps)
    grad_kv = return_rows(grads_ext, tok_rows, back_reach)
    in_sum = all_sum[1:].reshape(2, shards, d_own // zs, ff_block).swapaxes(0, 1)
    in_piece = exchange(in_sum, place, grads_ext).swapaxes(0, 1)
    all_piece = jnp.concatenate(
        [all_sum[:1], in_piece.reshape(2, block_rows_out, ff_block)], axis=0
    )
    all_all = from_rep(all_piece)
    grad_query_lin = undo_rope(
        grad_queries.reshape(tok_rows, HEADS, HEAD_DIM), cosine, sine_table
    ).reshape(tok_rows, D)
    grad_key_lin = undo_rope(
        grad_kv[:, :kv_width].reshape(tok_rows, KV_HEADS, HEAD_DIM), cosine, sine_table
    ).reshape(tok_rows, kv_width)
    grad_qkv = jnp.concatenate([grad_query_lin, grad_key_lin, grad_kv[:, kv_width:]], axis=1)
    grad_b_qkv = jnp.sum(grad_qkv, axis=0)
    qkv_low = after(grad_qkv.astype(jnp.bfloat16), layer_out, out_sum)
    grad_attn_normed = jnp.einsum(
        "te,de->td", qkv_low, full_qkv, preferred_element_type=jnp.float32
    )
    grad_front, grad_attn_gain = rms_backward(grad_attn_normed, normed_attn, inv_attn, gain_attn)
    grad_input = grad_after + grad_front

    vectors = jnp.concatenate([grad_attn_gain, grad_b_qkv, grad_mlp_gain])
    vectors = vectors + swap(vectors, core_steps[0])
    ends = [0, D, 2 * D, 2 * D + kv_width, qkv_width + D, qkv_width + 2 * D]
    vectors = jnp.concatenate(
        [vectors[a:b].reshape(shards, -1) for a, b in zip(ends[:-1], ends[1:])], axis=1
    )
    vectors = pick(vectors.reshape(shards, CORES, zs, 1, -1), core, 1).astype(jnp.bfloat16)
    vector_len = vectors.shape[-1]
    piece_rows = d_own // CORES // zs
    below = 16 - piece_rows % 16
    vectors = jnp.pad(vectors, ((0, 0), (0, 0), (0, below - 1), (0, qkv_width - vector_len)))
    query_parts = half_sum(attn_input, qkv_low).reshape(shards, zs, piece_rows, qkv_width)
    query_parts = jnp.concatenate([query_parts, vectors], axis=2)
    query_sum = shard_scatter(query_parts.reshape(-1, qkv_width))
    out_sum = out_sum.reshape(zs, piece_rows, D)
    out_sum = jnp.pad(out_sum, ((0, 0), (0, below), (0, 0))).reshape(-1, D)
    parts = jnp.concatenate([query_sum.reshape(-1, qkv_width), out_sum], axis=1)
    y_halves = (2,) * len(y_steps)
    parts = scatter(parts.reshape(parts.shape[:1] + y_halves + (-1,)), place, y_steps, 1)
    piece = scatter(parts.reshape(z_halves + (-1, parts.shape[1])), place, z_steps)
    for index, step in enumerate(y_steps[::-1]):
        mine = jnp.expand_dims(piece, index + 1)
        got = jnp.expand_dims(swap(piece, step), index + 1)
        piece = ordered(mine, got, place, step, index + 1)
    piece = piece.reshape(piece.shape[0], -1)
    if by_tiles:
        final_gate, final_up, final_down = weights_in_place(all_all, shards, ff_own)
    attn_half = piece
    for index, step in enumerate(z_steps[::-1]):
        mine = jnp.expand_dims(attn_half, index)
        got = jnp.expand_dims(swap(attn_half, step), index)
        if by_tiles and index == 0:
            got = after(got, final_down)
        attn_half = ordered(mine, got, place, step, index)
    attn_half = attn_half.reshape(-1, attn_half.shape[-1])
    attn_other = swap(attn_half, core_steps[0])
    attn_all = ordered(attn_half, attn_other, place, core_steps[0])
    attn_all = attn_all.reshape(CORES * zs, piece_rows + below, qkv_width + D)
    vector_own = attn_all[:, piece_rows, :vector_len].reshape(-1).astype(jnp.float32)
    attn_all = attn_all[:, :piece_rows].reshape(d_own, qkv_width + D)
    edges = [0, D, D + kv_width, qkv_width, qkv_width + D]
    final_query, final_key, final_value, final_out = [
        attn_all[:, a:b].astype(jnp.float32) for a, b in zip(edges[:-1], edges[1:])
    ]
    final_gain, final_bq, final_bk, final_bv, final_mlp_gain = [
        vector_own[a:b] for a, b in zip(cuts[:-1], cuts[1:])
    ]

    if not by_tiles:
        kept = [slice(kept_of(index, ff_block, ff_own)[1], ff_block) for index in range(blocks)]
        down_all = from_block(all_all[:, :, 0])
        in_all = all_all[:, :, 1:].reshape(zs, blocks, 2, shards, d_own // zs, ff_block)

        def in_place(pieces):
            columns = []
            for owner in range(shards):
                for index in range(blocks):
                    whole = pieces[:, index, owner].reshape(d_own, ff_block)
                    columns.append(whole[:, kept[index]])
            return jnp.concatenate(columns, axis=1).astype(jnp.float32)

        final_down = jnp.concatenate(
            [down_all[:, index].reshape(ff_block, D)[kept[index]] for index in range(blocks)], axis=0
        ).astype(jnp.float32)
        final_gate = in_place(in_all[:, :, 0])
        final_up = in_place(in_all[:, :, 1])
    return (
        layer_out,
        grad_input,
        final_gain,
        final_query,
        final_bq,
        final_key,
        final_bk,
        final_value,
        final_bv,
        final_out,
        final_mlp_gain,
        final_gate,
        final_up,
        final_down,
    )


def solution(mesh):
    return jax.shard_map(
        per_device,
        mesh=mesh,
        in_specs=(
            P(("rep", "shard"), None),
            P(("rep", "shard")),
            P("shard"),
            P("shard", None),
            P("shard"),
            P("shard", None),
            P("shard"),
            P("shard", None),
            P("shard"),
            P("shard", None),
            P("shard"),
            P("shard", None),
            P("shard", None),
            P("shard", None),
            P(("rep", "shard"), None),
        ),
        out_specs=(
            P(("rep", "shard"), None),
            P(("rep", "shard"), None),
            P("shard"),
            P("shard", None),
            P("shard"),
            P("shard", None),
            P("shard"),
            P("shard", None),
            P("shard"),
            P("shard", None),
            P("shard"),
            P("shard", None),
            P("shard", None),
            P("shard", None),
        ),
        check_vma=False,
    )
```
